512 devices in a mesh: member: 32 (over z, core), tensor: 16 (over y, x).
Axes of the slice: x: 4, y: 4, z: 16, core: 2. Of those that a mesh axis runs over, the one named last changes fastest.
Arguments:
- tokens: bfloat16 [32768, 5120], P('member', 'tensor'), may hold values from -6 to 6
- ids: int32 [32768, 1], P('member'), may hold values from 0 to 255; in each aligned block of 1024 rows (0 to 1023, 1024 to 2047, ...) at most 8 rows name the same one
- place: int32 [256], replicated, may hold values from 0 to 255, each once
- base_key_value_weight: bfloat16 [5120, 2048], P('tensor'), may hold values from -0.125 to 0.125
- adapter_down_weight: bfloat16 [256, 5120, 128], P('member', 'tensor'), may hold values from -0.078125 to 0.078125
- adapter_up_weight: bfloat16 [256, 64, 2048], P('member', None, 'tensor'), may hold values from -0.75 to 0.75
Outputs:
- projected: bfloat16 [32768, 2048], P('member', 'tensor')
The draws below stay inside these ranges and needn't reach their ends.
Inputs may be any that keep to these rules, and one draw needn't show every extreme that they name: `ids`: within each aligned block of 1024 rows (the rows of one member index) no co-player id occurs more than 8 times. `place`: every stored slot is named by exactly one co-player.
All inputs are finite; a program needn't handle non-finite values.
Results may differ from the reference program's by a relative error of at most 0.02.
Values may be sent and summed in bfloat16 or wider, within the bound.
No kernel may reach another device: no remote copies, remote signals or barrier semaphores. Data moves between devices by JAX's collectives and lax.ppermute only.
A program may use at most 64 MiB of HBM per device.

```python
import math
import jax
import jax.numpy as jnp
import numpy as np
from jax import lax

MODEL_WIDTH = 5120
KEY_VALUE_WIDTH = 1024
ADAPTER_RANK = 64
ROW_DEV = 1024
ADAPTER_TOTAL = 256
ROWS = 32768
CAP = 8
N_MEMBER = 32
N_TENSOR = 16


def strengthened(array, stream_key, source, target, shards_of, factor):
    owner, partner = [(jnp.arange(array.shape[position]) // (array.shape[position] // shards_of)).reshape([-1 if axis == position else 1 for axis in range(array.ndim)]) for position in (source, target)]
    chosen = jax.random.permutation(stream_key, shards_of)[partner]
    strong = (owner == chosen) | (owner == (partner + shards_of // 2) % shards_of)
    return jnp.where(strong, factor * array, array)


def levels(stream_key, extent, shards, least, top_value):
    gain, own = 1.0, jax.random.fold_in(stream_key, 6)
    for dim, parts in shards:
        draws = jnp.exp(jax.random.uniform(jax.random.fold_in(own, dim), (parts,), jnp.float32, least / len(shards), top_value / len(shards)))
        gain = gain * jnp.repeat(draws, extent[dim] // parts).reshape([-1 if axis == dim else 1 for axis in range(len(extent))])
    return gain


def deal_out(stream_key, own, number, rows, number_of, top, most, lean):
    sequence = jax.random.permutation(stream_key, number_of)
    packed, usual = portions_of(number_of, rows * top, most, lean, True), portions_of(number_of, rows * top, most, lean, False)
    places = jnp.arange(number_of)

    def named(tallies, turn):
        used = int((tallies > 0).sum())
        fixed = max(1, used // 4)
        shifted = fixed + (places - fixed + turn * (used - fixed)) % max(1, number_of - fixed)
        return jnp.zeros((number_of,), jnp.int32).at[sequence[jnp.where(places < fixed, places, shifted)]].set(jnp.asarray(tallies, jnp.int32))

    tallies = jnp.where(number % 4 == 0, named(packed, number // 4), named(usual, number - number // 4 - 1))
    mixed = jax.random.permutation(jax.random.fold_in(own, 3), number_of)
    source_of, receiver = mixed[0:number_of // 2 * 2:2], mixed[1:number_of // 2 * 2:2]
    margin = jnp.minimum(tallies[source_of] - 1, most - tallies[receiver]) // 2
    margin = jnp.where((source_of == sequence[0]) | (receiver == sequence[0]) | (tallies[receiver] == 0), 0, jnp.maximum(margin, 0))
    shifted = jax.random.randint(jax.random.fold_in(own, 4), (number_of // 2,), 0, 1 << 20) % (margin + 1)
    tallies = tallies.at[source_of].add(-shifted).at[receiver].add(shifted)
    labels = jnp.searchsorted(jnp.cumsum(tallies), jnp.arange(rows * top), side="right").astype(jnp.int32)
    listing = labels.reshape(top, rows).T
    listing = listing[jax.random.permutation(jax.random.fold_in(own, 1), rows)]
    turn = jax.random.randint(jax.random.fold_in(own, 2), (rows, 1), 0, top)
    return jnp.take_along_axis(listing, (jnp.arange(top)[None, :] + turn) % top, axis=1)


def portions_of(amount, total, reach, lean, full):
    portions = [(1 << 20) // math.isqrt(grade ** lean) + 1 for grade in range(1, amount + 1)]
    largest = reach if full else min(reach, max(-(-total // amount), total * portions[0] // sum(portions)))
    least = 1 if total - largest >= amount - 1 else 0
    counts, rest = [largest] + [least] * (amount - 1), total - largest - least * (amount - 1)
    while rest > 0:
        movable = [i for i in range(1, amount) if counts[i] < largest] or [i for i in range(1, amount) if counts[i] < reach]
        mass, budget = sum([portions[i] for i in movable]), rest
        for i in movable:
            addition = min(reach - counts[i], max(1, budget * portions[i] // mass), rest)
            counts[i] = counts[i] + addition
            rest = rest - addition
    return np.array(counts)


def centred(stream_key, extent, deviation, reach, pieces=(), held_as=jnp.bfloat16):
    factor_of = levels(stream_key, extent, pieces, -0.22, 0.18) if pieces else 1.0
    result = jax.random.normal(stream_key, extent, jnp.float32) * deviation * factor_of
    return jnp.minimum(jnp.maximum(result, -reach), reach).astype(held_as)


def gaussian_with(key, shape, spread, most, split, heavy, kind=jnp.bfloat16):
    drawn = spread * jax.random.normal(key, shape, jnp.float32)
    if split:
        drawn = drawn * levels(key, shape, split, -0.22, 0.18)
    return jnp.clip(strengthened(drawn, jax.random.fold_in(key, 3), *heavy), -most, most).astype(kind)


def setup_inputs(seed: int = 0) -> dict:
    key_list = jax.random.split(jax.random.key(seed), 7)
    tokens = centred(key_list[0], (ROWS, MODEL_WIDTH), 1.0, 6.0, ((0, 32), (1, 16)))
    ids_keys = jax.random.split(jax.random.fold_in(key_list[1], 1), ROWS // ROW_DEV)
    ids_turns = jax.random.permutation(jax.random.fold_in(key_list[1], 3), ROWS // ROW_DEV)
    ids = jax.vmap(lambda own, number: deal_out(jax.random.fold_in(key_list[1], 2), own, number, ROW_DEV, ADAPTER_TOTAL, 1, CAP, 2))(ids_keys, ids_turns).reshape((ROWS, 1))
    place = jax.random.permutation(key_list[2], ADAPTER_TOTAL).astype(jnp.int32)
    base_key_value_weight = gaussian_with(key_list[3], (MODEL_WIDTH, 2 * KEY_VALUE_WIDTH), MODEL_WIDTH ** -0.5, 0.125, ((0, 16),), (0, 1, 16, 2.0))
    adapter_down_weight = centred(key_list[4], (ADAPTER_TOTAL, MODEL_WIDTH, 2 * ADAPTER_RANK), MODEL_WIDTH ** -0.5, 0.078125, ((0, 32), (1, 16)))
    adapter_up_weight = centred(key_list[5], (ADAPTER_TOTAL, ADAPTER_RANK, 2 * KEY_VALUE_WIDTH), ADAPTER_RANK ** -0.5, 0.75, ((0, 32), (2, 16)))
    return dict(tokens=tokens, ids=ids, place=place, base_key_value_weight=base_key_value_weight, adapter_down_weight=adapter_down_weight, adapter_up_weight=adapter_up_weight)


def reference(tokens, ids, place, base_key_value_weight, adapter_down_weight, adapter_up_weight):
    row_number_total = tokens.shape[0]
    share_width = MODEL_WIDTH // N_TENSOR
    base_product = jnp.zeros((row_number_total, 2 * KEY_VALUE_WIDTH), jnp.float32)
    for shard in range(N_TENSOR):
        partial_value = jnp.dot(tokens[:, shard * share_width:(shard + 1) * share_width],
                          base_key_value_weight[shard * share_width:(shard + 1) * share_width],
                          preferred_element_type=jnp.float32).astype(jnp.bfloat16)
        partial_value = lax.optimization_barrier(partial_value)
        base_product = base_product + partial_value.astype(jnp.float32)
    stored_slot = place[ids[:, 0]].astype(jnp.int32)
    padded = jnp.concatenate([tokens, jnp.zeros((1, MODEL_WIDTH), tokens.dtype)], axis=0)
    most_rows = CAP * N_MEMBER

    def rows_by_adapter(adapter_product, adapter_slot):
        selected_slot = jnp.nonzero(stored_slot == adapter_slot, size=most_rows, fill_value=row_number_total)[0].astype(jnp.int32)
        selected_rows = padded[selected_slot]
        reduced_rank_rows = jnp.dot(selected_rows, adapter_down_weight[adapter_slot], preferred_element_type=jnp.float32).astype(jnp.bfloat16)
        up_projection_weight = adapter_up_weight[adapter_slot]
        key_part = jnp.dot(reduced_rank_rows[:, :ADAPTER_RANK], up_projection_weight[:, :KEY_VALUE_WIDTH], preferred_element_type=jnp.float32)
        value_part = jnp.dot(reduced_rank_rows[:, ADAPTER_RANK:], up_projection_weight[:, KEY_VALUE_WIDTH:], preferred_element_type=jnp.float32)
        adapter_correction = jnp.concatenate([key_part, value_part], axis=1).astype(jnp.bfloat16)
        return adapter_product.at[selected_slot].set(adapter_correction), None

    adapter_delta, discarded_output = lax.scan(rows_by_adapter, jnp.zeros((row_number_total + 1, 2 * KEY_VALUE_WIDTH), jnp.bfloat16),
                                      jnp.arange(ADAPTER_TOTAL, dtype=jnp.int32))
    return (base_product + adapter_delta[:row_number_total].astype(jnp.float32)).astype(jnp.bfloat16)
```

```python
import functools

import jax
import jax.numpy as jnp
from jax import lax
from jax.experimental import pallas as pl
from jax.experimental.pallas import tpu as pltpu
from jax.sharding import PartitionSpec as P

BF = jnp.bfloat16
F32 = jnp.float32
LANES = 128


def whole():
    return pl.BlockSpec(memory_space=pltpu.VMEM)


def cost(flops, size):
    return pl.CostEstimate(flops=flops, bytes_accessed=size, transcendentals=0)


def dispatch_kernel(cap, per_step, ids_ref, place_ref, tokens_ref, out_ref, dest_ref):
    rows = tokens_ref.shape[0]
    adapters = place_ref.shape[0]
    step = pl.program_id(0)

    @pl.when(step == 0)
    def _():
        hit = lax.broadcasted_iota(jnp.int32, (adapters, rows), 0) == ids_ref[...]
        hit_f = hit.astype(F32)
        before = lax.broadcasted_iota(jnp.int32, (rows, rows), 0) < lax.broadcasted_iota(jnp.int32, (rows, rows), 1)
        count = jnp.dot(hit_f.astype(BF), before.astype(F32).astype(BF), preferred_element_type=F32)
        value = count + place_ref[...].astype(F32) * cap
        dest_ref[...] = jnp.sum(hit_f * value, axis=0, keepdims=True).astype(jnp.int32)

    width = 64
    slots = per_step * width
    row_of = lax.broadcasted_iota(jnp.int32, (slots, rows), 0) + step * slots
    pick = (row_of == dest_ref[...]).astype(F32).astype(BF)
    moved = jnp.dot(pick, tokens_ref[...], preferred_element_type=F32)
    for d in range(per_step):
        own = moved[d * width:(d + 1) * width]
        out_ref[d, 0:64, :] = own[:, 0:128].astype(BF)
        out_ref[d, 64:128, :] = own[:, 128:256].astype(BF)
        out_ref[d, 128:160, :] = jnp.concatenate([own[0:32, 256:320], own[32:64, 256:320]], axis=1).astype(BF)


def dispatch(ids_row, place_col, tokens, members, cap):
    rows, feats = tokens.shape
    per_step = 4
    return pl.pallas_call(
        functools.partial(dispatch_kernel, cap, per_step),
        grid=(members // per_step,),
        in_specs=[
            pl.BlockSpec((1, rows), lambda i: (0, 0)),
            pl.BlockSpec(place_col.shape, lambda i: (0, 0)),
            pl.BlockSpec((rows, feats), lambda i: (0, 0)),
        ],
        out_specs=[
            pl.BlockSpec((per_step, 160, LANES), lambda i: (i, 0, 0)),
            pl.BlockSpec((1, rows), lambda i: (0, 0)),
        ],
        out_shape=[
            jax.ShapeDtypeStruct((members, 160, LANES), BF),
            jax.ShapeDtypeStruct((1, rows), jnp.int32),
        ],
        compiler_params=pltpu.CompilerParams(vmem_limit_bytes=40 << 20),
        cost_estimate=cost(2 * 2048 * 1024 * 320, 3 << 20),
        name="dispatch",
    )(ids_row, place_col, tokens)


def base_kernel(tokens_ref, weight_ref, out_ref):
    y = jnp.dot(tokens_ref[...], weight_ref[...], preferred_element_type=F32)
    out_ref[0] = y[:, :LANES].astype(BF)
    out_ref[1] = y[:, LANES:].astype(BF)


def base_product(tokens, weight):
    rows, feats = tokens.shape
    cols = weight.shape[1]
    return pl.pallas_call(
        base_kernel,
        grid=(cols // 256,),
        in_specs=[
            pl.BlockSpec((rows, feats), lambda i: (0, 0)),
            pl.BlockSpec((feats, 256), lambda i: (0, i)),
        ],
        out_specs=pl.BlockSpec((2, rows, LANES), lambda i: (i, 0, 0)),
        out_shape=jax.ShapeDtypeStruct((cols // LANES, rows, LANES), BF),
        compiler_params=pltpu.CompilerParams(vmem_limit_bytes=40 << 20),
        cost_estimate=cost(2 * rows * feats * cols, 6 << 20),
        name="base",
    )(tokens, weight)


def down_kernel(in_ref, down_ref, out_ref, low_ref):
    members = in_ref.shape[0]
    zero = jnp.zeros((64, 2 * LANES), BF)
    for pair in range(4):
        a, b = down_ref[2 * pair], down_ref[2 * pair + 1]
        both = jnp.concatenate([a, b], axis=1)
        tail = [both[256:320], zero] if pair < 2 else [zero, both[256:320]]
        x1 = in_ref[:, pair * 16:pair * 16 + 16, :].reshape(members * 16, LANES)
        x2 = in_ref[:, 64 + pair * 16:80 + pair * 16, :].reshape(members * 16, LANES)
        third = 128 + (pair % 2) * 16
        x3 = in_ref[:, third:third + 16, :].reshape(members * 16, LANES)
        y = jnp.dot(x1, both[0:128], preferred_element_type=F32)
        y += jnp.dot(x2, both[128:256], preferred_element_type=F32)
        y += jnp.dot(x3, jnp.concatenate(tail, axis=0), preferred_element_type=F32)
        first = lax.broadcasted_iota(jnp.int32, (members * 16, LANES), 0) % 16 < 8
        low_ref[pair] = jnp.where(first, y[:, :LANES], y[:, LANES:])
        for q in range(4):
            for i in range(4):
                out_ref[pair * 4 + q, i * members:(i + 1) * members, :] = low_ref[
                    pair, pl.ds(q * 4 + i, members, stride=16), :
                ].astype(BF)


def down_product(incoming, down):
    members = incoming.shape[0]
    return pl.pallas_call(
        down_kernel,
        in_specs=[whole(), whole()],
        out_specs=whole(),
        out_shape=jax.ShapeDtypeStruct((16, 4 * members, LANES), BF),
        scratch_shapes=[pltpu.VMEM((4, members * 16, LANES), F32)],
        compiler_params=pltpu.CompilerParams(vmem_limit_bytes=40 << 20),
        cost_estimate=cost(2 * 2048 * 320 * 256, 3 << 20),
        name="down",
    )(incoming, down)


def combine_kernel(dest_ref, delta_ref, base_ref, out_ref):
    rows = out_ref.shape[0]
    slots = delta_ref.shape[0]
    pick = (lax.broadcasted_iota(jnp.int32, (rows, slots), 1) == dest_ref[...]).astype(F32).astype(BF)
    delta = jnp.dot(pick, delta_ref[...], preferred_element_type=F32)
    out_ref[...] = (base_ref[...].astype(F32) + delta).astype(BF)


def combine(dest_col, delta, base):
    rows = dest_col.shape[0]
    block = 256
    return pl.pallas_call(
        combine_kernel,
        grid=(rows // block,),
        in_specs=[
            pl.BlockSpec((block, 1), lambda i: (i, 0)),
            pl.BlockSpec(delta.shape, lambda i: (0, 0)),
            pl.BlockSpec((block, LANES), lambda i: (i, 0)),
        ],
        out_specs=pl.BlockSpec((block, LANES), lambda i: (i, 0)),
        out_shape=jax.ShapeDtypeStruct((rows, LANES), BF),
        compiler_params=pltpu.CompilerParams(vmem_limit_bytes=40 << 20),
        cost_estimate=cost(2 * rows * 2048 * LANES, 1 << 20),
        name="combine",
    )(dest_col, delta, base)


def on_device(tokens, ids, place, base_weight, down, up):
    rows, feats = tokens.shape
    members = lax.axis_size("member")
    tensors = lax.axis_size("tensor")
    own_adapters = down.shape[0]
    rank = up.shape[1]
    cap = 8

    outbound, dest_row = dispatch(ids.reshape(1, rows), place.reshape(-1, 1), tokens, members, cap)
    incoming = lax.all_to_all(outbound, "member", 0, 0, tiled=True)
    partials = base_product(tokens, base_weight)
    base = lax.psum_scatter(partials, "tensor", scatter_dimension=0, tiled=True).reshape(rows, LANES)
    up_all = lax.all_gather(up, "member", axis=0, tiled=True)

    partial_low = down_product(incoming, down)
    shares = lax.all_to_all(partial_low, "tensor", 0, 0, tiled=True)
    low = jnp.sum(shares.astype(F32), axis=0).astype(BF)
    low = low.reshape(4, members, LANES).transpose(1, 0, 2)
    back = lax.all_to_all(low, "member", 0, 0, tiled=True).reshape(members * 4, LANES)
    key = jnp.concatenate([back[:64, :rank], back[64:, :rank]], axis=1)
    val = jnp.concatenate([back[:64, rank:], back[64:, rank:]], axis=1)
    half = tensors // 2
    send = jnp.concatenate([
        jnp.broadcast_to(key[None], (half,) + key.shape),
        jnp.broadcast_to(val[None], (half,) + val.shape),
    ])
    got = lax.all_to_all(send, "tensor", 0, 0, tiled=True)
    got = got.reshape(own_adapters, 2, members // 2, 4, 2, rank)
    low_rows = got.transpose(4, 2, 0, 1, 3, 5).reshape(members * own_adapters, cap, rank)
    delta = jnp.einsum("acr,ark->ack", low_rows, up_all, preferred_element_type=F32).astype(BF)
    delta = delta.reshape(members * own_adapters * cap, LANES)
    return combine(dest_row.reshape(rows, 1), delta, base)


def solution(mesh):
    in_specs = (
        P("member", "tensor"),
        P("member", None),
        P(),
        P("tensor", None),
        P("member", "tensor", None),
        P("member", None, "tensor"),
    )
    return jax.shard_map(on_device, mesh=mesh, in_specs=in_specs, out_specs=P("member", "tensor"), check_vma=False)
```

```python
import functools

import jax
import jax.numpy as jnp
from jax import lax
from jax.experimental import pallas as pl
from jax.experimental.pallas import tpu as pltpu
from jax.sharding import PartitionSpec as P

BF = jnp.bfloat16
F32 = jnp.float32
LANES = 128


def whole():
    return pl.BlockSpec(memory_space=pltpu.VMEM)


def cost(flops, size):
    return pl.CostEstimate(flops=flops, bytes_accessed=size, transcendentals=0)


def one_hot(at, index):
    return jnp.where(at == index, jnp.ones((), BF), jnp.zeros((), BF))


def within(dest, first):
    place = dest - first
    return jnp.where((place >= 0) & (place < 256), place, -1).astype(F32).astype(BF)


def dispatch_kernel(cap, ids_ref, place_ref, tokens_ref, out_ref, dest_ref, at_ref):
    rows = tokens_ref.shape[1]
    adapters = place_ref.shape[1]
    step = pl.program_id(0)

    @pl.when(step == 0)
    def _():
        hit = (lax.broadcasted_iota(jnp.int32, (adapters, rows), 0) == ids_ref[...]).astype(F32)
        before = lax.broadcasted_iota(jnp.int32, (rows, rows), 0) < lax.broadcasted_iota(jnp.int32, (rows, rows), 1)
        count = jnp.dot(hit.astype(BF), before.astype(F32).astype(BF), preferred_element_type=F32)
        rank = jnp.sum(hit * count, axis=0, keepdims=True)
        slot = jnp.dot(place_ref[...].astype(F32).astype(BF), hit.astype(BF), preferred_element_type=F32)
        dest_ref[...] = (slot[0:1] * cap + rank).astype(jnp.int32)
        at_ref[...] = lax.broadcasted_iota(jnp.int32, (256, rows), 0).astype(F32).astype(BF)

    width = 64
    per_step = out_ref.shape[0]
    for part in range(per_step * width // 256):
        pick = one_hot(at_ref[...], within(dest_ref[...], step * per_step * width + part * 256))
        moved = lax.dot_general(pick, tokens_ref[...], (((1,), (1,)), ((), ())), preferred_element_type=F32)
        for d in range(256 // width):
            own = moved[d * width:(d + 1) * width]
            to = part * (256 // width) + d
            out_ref[to, 0:64, :] = own[:, 0:128].astype(BF)
            out_ref[to, 64:128, :] = own[:, 128:256].astype(BF)
            out_ref[to, 128:160, :] = jnp.concatenate([own[0:32, 256:320], own[32:64, 256:320]], axis=1).astype(BF)


def dispatch(ids_row, place_row, tokens, members, cap):
    feats, rows = tokens.shape
    per_step = 8
    return pl.pallas_call(
        functools.partial(dispatch_kernel, cap),
        grid=(members // per_step,),
        in_specs=[
            pl.BlockSpec((1, rows), lambda i: (0, 0)),
            pl.BlockSpec(place_row.shape, lambda i: (0, 0)),
            pl.BlockSpec((feats, rows), lambda i: (0, 0)),
        ],
        out_specs=[
            pl.BlockSpec((per_step, 160, LANES), lambda i: (i, 0, 0)),
            pl.BlockSpec((1, rows), lambda i: (0, 0)),
        ],
        out_shape=[
            jax.ShapeDtypeStruct((members, 160, LANES), BF),
            jax.ShapeDtypeStruct((1, rows), jnp.int32),
        ],
        scratch_shapes=[pltpu.VMEM((256, rows), BF)],
        compiler_params=pltpu.CompilerParams(vmem_limit_bytes=58 << 20),
        cost_estimate=cost(2 * 2048 * 1024 * 320, 3 << 20),
        name="dispatch",
    )(ids_row, place_row, tokens)


def base_kernel(dest_ref, tokens_ref, weight_ref, out_ref, rows_ref):
    @pl.when(pl.program_id(0) == 0)
    def _():
        rows_ref[...] = tokens_ref[...].T

    y = jnp.dot(rows_ref[...], weight_ref[...], preferred_element_type=F32)
    out_ref[0] = y[:, :LANES].astype(BF)
    out_ref[1] = y[:, LANES:].astype(BF)


def base_product(dest_row, tokens, weight):
    feats, rows = tokens.shape
    cols = weight.shape[1]
    return pl.pallas_call(
        base_kernel,
        grid=(cols // 256,),
        in_specs=[
            pl.BlockSpec((1, rows), lambda i: (0, 0)),
            pl.BlockSpec((feats, rows), lambda i: (0, 0)),
            pl.BlockSpec((feats, 256), lambda i: (0, i)),
        ],
        out_specs=pl.BlockSpec((2, rows, LANES), lambda i: (i, 0, 0)),
        out_shape=jax.ShapeDtypeStruct((cols // LANES, rows, LANES), BF),
        scratch_shapes=[pltpu.VMEM((rows, feats), BF)],
        compiler_params=pltpu.CompilerParams(vmem_limit_bytes=40 << 20),
        cost_estimate=cost(2 * rows * feats * cols, 6 << 20),
        name="base",
    )(dest_row, tokens, weight)


def down_kernel(in_ref, down_ref, out_ref):
    members = in_ref.shape[0]
    zero = jnp.zeros((64, 2 * LANES), BF)
    first = lax.broadcasted_iota(jnp.int32, (members * 16, LANES), 0) % 16 < 8
    for pair in range(4):
        both = jnp.concatenate([down_ref[2 * pair], down_ref[2 * pair + 1]], axis=1)
        tail = [both[256:320], zero] if pair < 2 else [zero, both[256:320]]
        x1 = in_ref[:, pair * 16:pair * 16 + 16, :].reshape(members * 16, LANES)
        x2 = in_ref[:, 64 + pair * 16:80 + pair * 16, :].reshape(members * 16, LANES)
        third = 128 + (pair % 2) * 16
        x3 = in_ref[:, third:third + 16, :].reshape(members * 16, LANES)
        y = jnp.dot(x1, both[0:128], preferred_element_type=F32)
        y += jnp.dot(x2, both[128:256], preferred_element_type=F32)
        y += jnp.dot(x3, jnp.concatenate(tail, axis=0), preferred_element_type=F32)
        low = jnp.where(first, y[:, :LANES], y[:, LANES:]).astype(BF)
        out_ref[:, pair * 16:pair * 16 + 16, :] = low.reshape(members, 16, LANES)


def down_product(incoming, down):
    members = incoming.shape[0]
    return pl.pallas_call(
        down_kernel,
        in_specs=[whole(), whole()],
        out_specs=whole(),
        out_shape=jax.ShapeDtypeStruct((members, 64, LANES), BF),
        compiler_params=pltpu.CompilerParams(vmem_limit_bytes=40 << 20),
        cost_estimate=cost(3 * 10**10, 3 << 20),
        name="down",
    )(incoming, down)


def combine_kernel(dest_ref, delta_ref, base_ref, out_ref):
    rows = out_ref.shape[0]
    slots = delta_ref.shape[0]
    at = lax.broadcasted_iota(jnp.int32, (rows, 256), 1).astype(F32).astype(BF)
    total = base_ref[...].astype(F32)
    for part in range(slots // 256):
        pick = one_hot(at, within(dest_ref[...], part * 256))
        total += jnp.dot(pick, delta_ref[part * 256:(part + 1) * 256, :], preferred_element_type=F32)
    out_ref[...] = total.astype(out_ref.dtype)


def combine(dest_col, delta, base):
    rows = dest_col.shape[0]
    block = 512
    return pl.pallas_call(
        combine_kernel,
        grid=(rows // block,),
        in_specs=[
            pl.BlockSpec((block, 1), lambda i: (i, 0)),
            pl.BlockSpec(delta.shape, lambda i: (0, 0)),
            pl.BlockSpec((block, LANES), lambda i: (i, 0)),
        ],
        out_specs=pl.BlockSpec((block, LANES), lambda i: (i, 0)),
        out_shape=jax.ShapeDtypeStruct((rows, LANES), BF),
        compiler_params=pltpu.CompilerParams(vmem_limit_bytes=40 << 20),
        cost_estimate=cost(2 * rows * 2048 * LANES, 1 << 20),
        name="combine",
    )(dest_col, delta, base)


def up_kernel(low_ref, up_ref, out_ref):
    chips = low_ref.shape[0]
    rank = up_ref.shape[1]
    zero = jnp.zeros((rank, 2 * LANES), BF)
    first = lax.broadcasted_iota(jnp.int32, (chips * 16, LANES), 0) % 16 < 8
    for pair in range(up_ref.shape[0] // 2):
        both = jnp.concatenate([up_ref[2 * pair], up_ref[2 * pair + 1]], axis=1)
        weight = jnp.concatenate(
            [jnp.concatenate([both, zero], axis=1), jnp.concatenate([zero, both], axis=1)], axis=0
        )
        x = low_ref[:, pair * 16:pair * 16 + 16, :].reshape(chips * 16, LANES)
        y = jnp.dot(x, weight, preferred_element_type=F32)
        for core in range(2):
            at = 2 * LANES * core
            delta = jnp.where(first, y[:, at:at + LANES], y[:, at + LANES:at + 2 * LANES]).astype(BF)
            out_ref[:, core, pair * 16:pair * 16 + 16, :] = delta.reshape(chips, 16, LANES)


def up_product(low, up):
    chips, slots, _ = low.shape
    return pl.pallas_call(
        up_kernel,
        in_specs=[whole(), whole()],
        out_specs=whole(),
        out_shape=jax.ShapeDtypeStruct((chips, 2, slots, LANES), BF),
        compiler_params=pltpu.CompilerParams(vmem_limit_bytes=40 << 20),
        cost_estimate=cost(2 * 1024 * 128 * 512, 1 << 20),
        name="up",
    )(low, up)


def on_device(tokens, ids, place, base_weight, down, up):
    rows, feats = tokens.shape
    members = lax.axis_size("member")
    tensors = lax.axis_size("tensor")
    chips = members // 2
    own_adapters = down.shape[0]
    rank = up.shape[1]
    cap = 8
    rest = own_adapters * cap

    outbound, dest_row = dispatch(ids.reshape(1, rows), place.reshape(1, -1), tokens.T, members, cap)
    incoming = lax.all_to_all(outbound, "member", 0, 0, tiled=True)
    partials = base_product(dest_row, tokens.T, base_weight)
    base = lax.psum_scatter(partials, "tensor", scatter_dimension=0, tiled=True).reshape(rows, LANES)

    partial_low = down_product(incoming, down).reshape(tensors, 2 * rest, LANES)
    shares = lax.all_to_all(partial_low, "tensor", 0, 0, tiled=True)
    low = jnp.sum(shares.astype(F32), axis=0).astype(BF)
    key = jnp.concatenate([low[:rest, :rank], low[rest:, :rank]], axis=1)
    val = jnp.concatenate([low[:rest, rank:], low[rest:, rank:]], axis=1)
    half = tensors // 2
    send = jnp.concatenate([
        jnp.broadcast_to(key[None], (half,) + key.shape),
        jnp.broadcast_to(val[None], (half,) + val.shape),
    ])
    got = lax.all_to_all(send, "tensor", 0, 0, tiled=True)
    delta = up_product(got, up).reshape(members, rest, LANES)
    back = lax.all_to_all(delta, "member", 0, 0, tiled=True).reshape(members * rest, LANES)
    return combine(dest_row.reshape(rows, 1), back, base)


def solution(mesh):
    in_specs = (
        P("member", "tensor"),
        P("member", None),
        P(),
        P("tensor", None),
        P("member", "tensor", None),
        P("member", None, "tensor"),
    )
    return jax.shard_map(on_device, mesh=mesh, in_specs=in_specs, out_specs=P("member", "tensor"), check_vma=False)
```

```python
import functools

import jax
import jax.numpy as jnp
from jax import lax
from jax.experimental import pallas as pl
from jax.experimental.pallas import tpu as pltpu
from jax.sharding import PartitionSpec as P

BF = jnp.bfloat16
F32 = jnp.float32
LANES = 128


def whole():
    return pl.BlockSpec(memory_space=pltpu.VMEM)


def cost(flops, size):
    return pl.CostEstimate(flops=flops, bytes_accessed=size, transcendentals=0)


def one_hot(at, index):
    return jnp.where(at == index, jnp.ones((), BF), jnp.zeros((), BF))


def within(dest, first):
    place = dest - first
    return jnp.where((place >= 0) & (place < 256), place, -1).astype(F32).astype(BF)


def dispatch_kernel(cap, ids_ref, place_ref, tokens_ref, out_ref, dest_ref, at_ref):
    rows = tokens_ref.shape[1]
    adapters = place_ref.shape[1]
    step = pl.program_id(0)

    @pl.when(step == 0)
    def _():
        hit = (lax.broadcasted_iota(jnp.int32, (adapters, rows), 0) == ids_ref[...]).astype(F32)
        before = lax.broadcasted_iota(jnp.int32, (rows, rows), 0) < lax.broadcasted_iota(jnp.int32, (rows, rows), 1)
        count = jnp.dot(hit.astype(BF), before.astype(F32).astype(BF), preferred_element_type=F32)
        rank = jnp.sum(hit * count, axis=0, keepdims=True)
        slot = jnp.dot(place_ref[...].astype(F32).astype(BF), hit.astype(BF), preferred_element_type=F32)
        dest_ref[...] = (slot[0:1] * cap + rank).astype(jnp.int32)
        at_ref[...] = lax.broadcasted_iota(jnp.int32, (256, rows), 0).astype(F32).astype(BF)

    width = 64
    per_step = out_ref.shape[0]
    for part in range(per_step * width // 256):
        pick = one_hot(at_ref[...], within(dest_ref[...], step * per_step * width + part * 256))
        moved = lax.dot_general(pick, tokens_ref[...], (((1,), (1,)), ((), ())), preferred_element_type=F32)
        for d in range(256 // width):
            own = moved[d * width:(d + 1) * width]
            to = part * (256 // width) + d
            out_ref[to, 0:64, :] = own[:, 0:128].astype(BF)
            out_ref[to, 64:128, :] = own[:, 128:256].astype(BF)
            out_ref[to, 128:160, :] = jnp.concatenate([own[0:32, 256:320], own[32:64, 256:320]], axis=1).astype(BF)


def dispatch(ids_row, place_row, tokens, members, cap):
    feats, rows = tokens.shape
    per_step = 8
    return pl.pallas_call(
        functools.partial(dispatch_kernel, cap),
        grid=(members // per_step,),
        in_specs=[
            pl.BlockSpec((1, rows), lambda i: (0, 0)),
            pl.BlockSpec(place_row.shape, lambda i: (0, 0)),
            pl.BlockSpec((feats, rows), lambda i: (0, 0)),
        ],
        out_specs=[
            pl.BlockSpec((per_step, 160, LANES), lambda i: (i, 0, 0)),
            pl.BlockSpec((1, rows), lambda i: (0, 0)),
        ],
        out_shape=[
            jax.ShapeDtypeStruct((members, 160, LANES), BF),
            jax.ShapeDtypeStruct((1, rows), jnp.int32),
        ],
        scratch_shapes=[pltpu.VMEM((256, rows), BF)],
        compiler_params=pltpu.CompilerParams(vmem_limit_bytes=58 << 20),
        cost_estimate=cost(2 * 2048 * 1024 * 320, 3 << 20),
        name="dispatch",
    )(ids_row, place_row, tokens)


def base_kernel(position_ref, dest_ref, tokens_ref, weight_ref, *out_refs):
    rows = tokens_ref[...].T
    half = rows.shape[0] // 2
    own = position_ref[0]
    odd = own % 2 == 1
    for pair in range(8):
        at = pl.multiple_of((own // 2 ^ pair) * 2 * LANES, 2 * LANES)
        y = jnp.dot(rows, weight_ref[:, pl.ds(at, 2 * LANES)], preferred_element_type=F32).astype(BF)
        for n in range(2):
            block = jnp.where(odd == (n == 1), y[:, :LANES], y[:, LANES:])
            l, k = divmod(2 * pair + n, 4)
            out_refs[k][l] = block[:half]
            out_refs[4 + l][k] = block[half:]


def base_product(position, dest_row, tokens, weight):
    feats, rows = tokens.shape
    cols = weight.shape[1]
    return pl.pallas_call(
        base_kernel,
        in_specs=[pl.BlockSpec(memory_space=pltpu.SMEM), whole(), whole(), whole()],
        out_specs=[whole()] * 8,
        out_shape=[jax.ShapeDtypeStruct((4, rows // 2, LANES), BF)] * 8,
        compiler_params=pltpu.CompilerParams(vmem_limit_bytes=24 << 20),
        cost_estimate=cost(2 * rows * feats * cols, 6 << 20),
        name="base",
    )(position, dest_row, tokens, weight)


def first_sum_kernel(*refs):
    for group in range(2):
        total = refs[4 * group][0].astype(F32)
        for ref in refs[4 * group + 1:4 * group + 4]:
            total += ref[0].astype(F32)
        entry = pl.program_id(0)
        for n in range(4):

            @pl.when(entry == n)
            def _(n=n, total=total, group=group):
                refs[8 + 4 * group + n][...] = total.astype(BF)


def first_sum(blocks):
    _, rows, _ = blocks[0].shape
    return pl.pallas_call(
        first_sum_kernel,
        grid=(4,),
        in_specs=[pl.BlockSpec((1, rows, LANES), lambda i: (i, 0, 0))] * 8,
        out_specs=[pl.BlockSpec((rows, LANES), lambda i: (0, 0))] * 8,
        out_shape=[jax.ShapeDtypeStruct((rows, LANES), BF)] * 8,
        compiler_params=pltpu.CompilerParams(vmem_limit_bytes=24 << 20),
        cost_estimate=cost(8 * rows * LANES * 4, 5 << 20),
        name="first_sum",
    )(*blocks)


def second_sum_kernel(*refs):
    rows = refs[0].shape[0]
    for group in range(2):
        total = refs[4 * group][...].astype(F32)
        for ref in refs[4 * group + 1:4 * group + 4]:
            total += ref[...].astype(F32)
        refs[8][group * rows:(group + 1) * rows, :] = total


def second_sum(blocks):
    rows = blocks[0].shape[0]
    return pl.pallas_call(
        second_sum_kernel,
        in_specs=[whole()] * 8,
        out_specs=whole(),
        out_shape=jax.ShapeDtypeStruct((2 * rows, LANES), F32),
        compiler_params=pltpu.CompilerParams(vmem_limit_bytes=16 << 20),
        cost_estimate=cost(8 * rows * LANES, 2 << 20),
        name="second_sum",
    )(*blocks)


def down_kernel(in_ref, down_ref, out_ref):
    members = in_ref.shape[0]
    zero = jnp.zeros((64, 2 * LANES), BF)
    first = lax.broadcasted_iota(jnp.int32, (members * 16, LANES), 0) % 16 < 8
    for pair in range(4):
        both = jnp.concatenate([down_ref[2 * pair], down_ref[2 * pair + 1]], axis=1)
        tail = [both[256:320], zero] if pair < 2 else [zero, both[256:320]]
        x1 = in_ref[:, pair * 16:pair * 16 + 16, :].reshape(members * 16, LANES)
        x2 = in_ref[:, 64 + pair * 16:80 + pair * 16, :].reshape(members * 16, LANES)
        third = 128 + (pair % 2) * 16
        x3 = in_ref[:, third:third + 16, :].reshape(members * 16, LANES)
        y = jnp.dot(x1, both[0:128], preferred_element_type=F32)
        y += jnp.dot(x2, both[128:256], preferred_element_type=F32)
        y += jnp.dot(x3, jnp.concatenate(tail, axis=0), preferred_element_type=F32)
        low = jnp.where(first, y[:, :LANES], y[:, LANES:]).astype(BF)
        out_ref[:, pair * 16:pair * 16 + 16, :] = low.reshape(members, 16, LANES)


def down_product(incoming, down):
    members = incoming.shape[0]
    return pl.pallas_call(
        down_kernel,
        in_specs=[whole(), whole()],
        out_specs=whole(),
        out_shape=jax.ShapeDtypeStruct((members, 64, LANES), BF),
        compiler_params=pltpu.CompilerParams(vmem_limit_bytes=24 << 20),
        cost_estimate=cost(3 * 10**10, 3 << 20),
        name="down",
    )(incoming, down)


def combine_kernel(dest_ref, delta_ref, base_ref, out_ref):
    rows = out_ref.shape[0]
    slots = delta_ref.shape[0]
    at = lax.broadcasted_iota(jnp.int32, (rows, 256), 1).astype(F32).astype(BF)
    total = base_ref[...].astype(F32)
    for part in range(slots // 256):
        pick = one_hot(at, within(dest_ref[...], part * 256))
        total += jnp.dot(pick, delta_ref[part * 256:(part + 1) * 256, :], preferred_element_type=F32)
    out_ref[...] = total.astype(out_ref.dtype)


def combine(dest_col, delta, base):
    rows = dest_col.shape[0]
    block = 512
    return pl.pallas_call(
        combine_kernel,
        grid=(rows // block,),
        in_specs=[
            pl.BlockSpec((block, 1), lambda i: (i, 0)),
            pl.BlockSpec(delta.shape, lambda i: (0, 0)),
            pl.BlockSpec((block, LANES), lambda i: (i, 0)),
        ],
        out_specs=pl.BlockSpec((block, LANES), lambda i: (i, 0)),
        out_shape=jax.ShapeDtypeStruct((rows, LANES), BF),
        compiler_params=pltpu.CompilerParams(vmem_limit_bytes=24 << 20),
        cost_estimate=cost(2 * rows * 2048 * LANES, 1 << 20),
        name="combine",
    )(dest_col, delta, base)


def up_kernel(low_ref, up_ref, out_ref):
    chips = low_ref.shape[0]
    rank = up_ref.shape[1]
    zero = jnp.zeros((rank, 2 * LANES), BF)
    first = lax.broadcasted_iota(jnp.int32, (chips * 16, LANES), 0) % 16 < 8
    for pair in range(up_ref.shape[0] // 2):
        both = jnp.concatenate([up_ref[2 * pair], up_ref[2 * pair + 1]], axis=1)
        weight = jnp.concatenate(
            [jnp.concatenate([both, zero], axis=1), jnp.concatenate([zero, both], axis=1)], axis=0
        )
        x = low_ref[:, pair * 16:pair * 16 + 16, :].reshape(chips * 16, LANES)
        y = jnp.dot(x, weight, preferred_element_type=F32)
        for core in range(2):
            at = 2 * LANES * core
            delta = jnp.where(first, y[:, at:at + LANES], y[:, at + LANES:at + 2 * LANES]).astype(BF)
            out_ref[:, core, pair * 16:pair * 16 + 16, :] = delta.reshape(chips, 16, LANES)


def up_product(low, up):
    chips, slots, _ = low.shape
    return pl.pallas_call(
        up_kernel,
        in_specs=[whole(), whole()],
        out_specs=whole(),
        out_shape=jax.ShapeDtypeStruct((chips, 2, slots, LANES), BF),
        compiler_params=pltpu.CompilerParams(vmem_limit_bytes=24 << 20),
        cost_estimate=cost(2 * 1024 * 128 * 512, 1 << 20),
        name="up",
    )(low, up)


def on_device(tokens, ids, place, base_weight, down, up):
    rows, feats = tokens.shape
    members = lax.axis_size("member")
    tensors = lax.axis_size("tensor")
    chips = members // 2
    own_adapters = down.shape[0]
    rank = up.shape[1]
    cap = 8
    rest = own_adapters * cap

    outbound, dest_row = dispatch(ids.reshape(1, rows), place.reshape(1, -1), tokens.T, members, cap)
    incoming = lax.all_to_all(outbound, "member", 0, 0, tiled=True)
    def swapped(array, flip):
        return lax.ppermute(array, "tensor", [(t, t ^ flip) for t in range(tensors)])

    position = lax.axis_index("tensor").astype(jnp.int32).reshape(1)
    partials = base_product(position, dest_row, tokens.T, base_weight)
    along_x = [partials[0]] + [swapped(partials[k], k) for k in range(1, 4)]
    along_y = [partials[4]] + [swapped(partials[4 + l], 4 * l) for l in range(1, 4)]
    sums = first_sum(along_x + along_y)
    incoming, *sums = lax.optimization_barrier((incoming, *sums))
    then_y = [sums[0]] + [swapped(sums[l], 4 * l) for l in range(1, 4)]
    then_x = [sums[4]] + [swapped(sums[4 + k], k) for k in range(1, 4)]
    base = second_sum(then_y + then_x)

    partial_low = down_product(incoming, down).reshape(tensors, 2 * rest, LANES)
    shares = lax.all_to_all(partial_low, "tensor", 0, 0, tiled=True)
    low = jnp.sum(shares.astype(F32), axis=0).astype(BF)
    key = jnp.concatenate([low[:rest, :rank], low[rest:, :rank]], axis=1)
    val = jnp.concatenate([low[:rest, rank:], low[rest:, rank:]], axis=1)
    half = tensors // 2
    send = jnp.concatenate([
        jnp.broadcast_to(key[None], (half,) + key.shape),
        jnp.broadcast_to(val[None], (half,) + val.shape),
    ])
    got = lax.all_to_all(send, "tensor", 0, 0, tiled=True)
    delta = up_product(got, up).reshape(members, rest, LANES)
    back = lax.all_to_all(delta, "member", 0, 0, tiled=True).reshape(members * rest, LANES)
    return combine(dest_row.reshape(rows, 1), back, base)


def solution(mesh):
    in_specs = (
        P("member", "tensor"),
        P("member", None),
        P(),
        P("tensor", None),
        P("member", "tensor", None),
        P("member", None, "tensor"),
    )
    return jax.shard_map(on_device, mesh=mesh, in_specs=in_specs, out_specs=P("member", "tensor"), check_vma=False)
```

```python
import functools

import jax
import jax.numpy as jnp
from jax import lax
from jax.experimental import pallas as pl
from jax.experimental.pallas import tpu as pltpu
from jax.sharding import PartitionSpec as P

BF = jnp.bfloat16
F32 = jnp.float32
LANES = 128


def whole():
    return pl.BlockSpec(memory_space=pltpu.VMEM)


def cost(flops, size):
    return pl.CostEstimate(flops=flops, bytes_accessed=size, transcendentals=0)


def one_hot(at, index):
    return jnp.where(at == index, jnp.ones((), BF), jnp.zeros((), BF))


def within(dest, first):
    place = dest - first
    return jnp.where((place >= 0) & (place < 256), place, -1).astype(F32).astype(BF)


def dispatch_kernel(cap, ids_ref, place_ref, tokens_ref, out_ref, dest_ref, at_ref):
    rows = tokens_ref.shape[1]
    adapters = place_ref.shape[1]
    step = pl.program_id(0)

    @pl.when(step == 0)
    def _():
        hit = (lax.broadcasted_iota(jnp.int32, (adapters, rows), 0) == ids_ref[...]).astype(F32)
        before = lax.broadcasted_iota(jnp.int32, (rows, rows), 0) < lax.broadcasted_iota(jnp.int32, (rows, rows), 1)
        count = jnp.dot(hit.astype(BF), before.astype(F32).astype(BF), preferred_element_type=F32)
        rank = jnp.sum(hit * count, axis=0, keepdims=True)
        slot = jnp.dot(place_ref[...].astype(F32).astype(BF), hit.astype(BF), preferred_element_type=F32)
        dest_ref[...] = (slot[0:1] * cap + rank).astype(jnp.int32)
        at_ref[...] = lax.broadcasted_iota(jnp.int32, (256, rows), 0).astype(F32).astype(BF)

    width = 64
    per_step = out_ref.shape[0]
    for part in range(per_step * width // 256):
        pick = one_hot(at_ref[...], within(dest_ref[...], step * per_step * width + part * 256))
        moved = lax.dot_general(pick, tokens_ref[...], (((1,), (1,)), ((), ())), preferred_element_type=F32)
        for d in range(256 // width):
            own = moved[d * width:(d + 1) * width]
            to = part * (256 // width) + d
            out_ref[to, 0:64, :] = own[:, 0:128].astype(BF)
            out_ref[to, 64:128, :] = own[:, 128:256].astype(BF)
            out_ref[to, 128:160, :] = jnp.concatenate([own[0:32, 256:320], own[32:64, 256:320]], axis=1).astype(BF)


def dispatch(ids_row, place_row, tokens, members, cap):
    feats, rows = tokens.shape
    per_step = 8
    return pl.pallas_call(
        functools.partial(dispatch_kernel, cap),
        grid=(members // per_step,),
        in_specs=[
            pl.BlockSpec((1, rows), lambda i: (0, 0)),
            pl.BlockSpec(place_row.shape, lambda i: (0, 0)),
            pl.BlockSpec((feats, rows), lambda i: (0, 0)),
        ],
        out_specs=[
            pl.BlockSpec((per_step, 160, LANES), lambda i: (i, 0, 0)),
            pl.BlockSpec((1, rows), lambda i: (0, 0)),
        ],
        out_shape=[
            jax.ShapeDtypeStruct((members, 160, LANES), BF),
            jax.ShapeDtypeStruct((1, rows), jnp.int32),
        ],
        scratch_shapes=[pltpu.VMEM((256, rows), BF)],
        compiler_params=pltpu.CompilerParams(vmem_limit_bytes=58 << 20),
        cost_estimate=cost(2 * 2048 * 1024 * 320, 3 << 20),
        name="dispatch",
    )(ids_row, place_row, tokens)


def base_kernel(position_ref, dest_ref, tokens_ref, weight_ref, *out_refs):
    rows = tokens_ref[...].T
    half = rows.shape[0] // 2
    own = position_ref[0]
    odd = own % 2 == 1
    for pair in range(8):
        at = pl.multiple_of((own // 2 ^ pair) * 2 * LANES, 2 * LANES)
        y = jnp.dot(rows, weight_ref[:, pl.ds(at, 2 * LANES)], preferred_element_type=F32).astype(BF)
        for n in range(2):
            block = jnp.where(odd == (n == 1), y[:, :LANES], y[:, LANES:])
            l, k = divmod(2 * pair + n, 4)
            out_refs[k][l] = block[:half]
            out_refs[4 + l][k] = block[half:]


def base_product(position, dest_row, tokens, weight):
    feats, rows = tokens.shape
    cols = weight.shape[1]
    return pl.pallas_call(
        base_kernel,
        in_specs=[pl.BlockSpec(memory_space=pltpu.SMEM), whole(), whole(), whole()],
        out_specs=[whole()] * 8,
        out_shape=[jax.ShapeDtypeStruct((4, rows // 2, LANES), BF)] * 8,
        compiler_params=pltpu.CompilerParams(vmem_limit_bytes=24 << 20),
        cost_estimate=cost(2 * rows * feats * cols, 6 << 20),
        name="base",
    )(position, dest_row, tokens, weight)


def first_sum_kernel(*refs):
    for group in range(2):
        total = refs[4 * group][0].astype(F32)
        for ref in refs[4 * group + 1:4 * group + 4]:
            total += ref[0].astype(F32)
        entry = pl.program_id(0)
        for n in range(4):

            @pl.when(entry == n)
            def _(n=n, total=total, group=group):
                refs[8 + 4 * group + n][...] = total.astype(BF)


def first_sum(blocks):
    _, rows, _ = blocks[0].shape
    return pl.pallas_call(
        first_sum_kernel,
        grid=(4,),
        in_specs=[pl.BlockSpec((1, rows, LANES), lambda i: (i, 0, 0))] * 8,
        out_specs=[pl.BlockSpec((rows, LANES), lambda i: (0, 0))] * 8,
        out_shape=[jax.ShapeDtypeStruct((rows, LANES), BF)] * 8,
        compiler_params=pltpu.CompilerParams(vmem_limit_bytes=24 << 20),
        cost_estimate=cost(8 * rows * LANES * 4, 5 << 20),
        name="first_sum",
    )(*blocks)


def second_sum_kernel(*refs):
    rows = refs[0].shape[0]
    for group in range(2):
        total = refs[4 * group][...].astype(F32)
        for ref in refs[4 * group + 1:4 * group + 4]:
            total += ref[...].astype(F32)
        refs[8][group * rows:(group + 1) * rows, :] = total


def second_sum(blocks):
    rows = blocks[0].shape[0]
    return pl.pallas_call(
        second_sum_kernel,
        in_specs=[whole()] * 8,
        out_specs=whole(),
        out_shape=jax.ShapeDtypeStruct((2 * rows, LANES), F32),
        compiler_params=pltpu.CompilerParams(vmem_limit_bytes=16 << 20),
        cost_estimate=cost(8 * rows * LANES, 2 << 20),
        name="second_sum",
    )(*blocks)


def down_kernel(in_ref, down_ref, out_ref):
    members = in_ref.shape[0]
    zero = jnp.zeros((64, 2 * LANES), BF)
    first = lax.broadcasted_iota(jnp.int32, (members * 16, LANES), 0) % 16 < 8
    for pair in range(4):
        both = jnp.concatenate([down_ref[2 * pair], down_ref[2 * pair + 1]], axis=1)
        tail = [both[256:320], zero] if pair < 2 else [zero, both[256:320]]
        x1 = in_ref[:, pair * 16:pair * 16 + 16, :].reshape(members * 16, LANES)
        x2 = in_ref[:, 64 + pair * 16:80 + pair * 16, :].reshape(members * 16, LANES)
        third = 128 + (pair % 2) * 16
        x3 = in_ref[:, third:third + 16, :].reshape(members * 16, LANES)
        y = jnp.dot(x1, both[0:128], preferred_element_type=F32)
        y += jnp.dot(x2, both[128:256], preferred_element_type=F32)
        y += jnp.dot(x3, jnp.concatenate(tail, axis=0), preferred_element_type=F32)
        low = jnp.where(first, y[:, :LANES], y[:, LANES:]).astype(BF)
        out_ref[:, pair * 16:pair * 16 + 16, :] = low.reshape(members, 16, LANES)


def down_product(incoming, down):
    members = incoming.shape[0]
    return pl.pallas_call(
        down_kernel,
        in_specs=[whole(), whole()],
        out_specs=whole(),
        out_shape=jax.ShapeDtypeStruct((members, 64, LANES), BF),
        compiler_params=pltpu.CompilerParams(vmem_limit_bytes=24 << 20),
        cost_estimate=cost(3 * 10**10, 3 << 20),
        name="down",
    )(incoming, down)


def combine_kernel(dest_ref, delta_ref, base_ref, out_ref):
    rows = out_ref.shape[0]
    slots = delta_ref.shape[0]
    at = lax.broadcasted_iota(jnp.int32, (rows, 256), 1).astype(F32).astype(BF)
    total = base_ref[...].astype(F32)
    for part in range(slots // 256):
        pick = one_hot(at, within(dest_ref[...], part * 256))
        total += jnp.dot(pick, delta_ref[part * 256:(part + 1) * 256, :], preferred_element_type=F32)
    out_ref[...] = total.astype(out_ref.dtype)


def combine(dest_col, delta, base):
    rows = dest_col.shape[0]
    block = 512
    return pl.pallas_call(
        combine_kernel,
        grid=(rows // block,),
        in_specs=[
            pl.BlockSpec((block, 1), lambda i: (i, 0)),
            pl.BlockSpec(delta.shape, lambda i: (0, 0)),
            pl.BlockSpec((block, LANES), lambda i: (i, 0)),
        ],
        out_specs=pl.BlockSpec((block, LANES), lambda i: (i, 0)),
        out_shape=jax.ShapeDtypeStruct((rows, LANES), BF),
        compiler_params=pltpu.CompilerParams(vmem_limit_bytes=24 << 20),
        cost_estimate=cost(2 * rows * 2048 * LANES, 1 << 20),
        name="combine",
    )(dest_col, delta, base)


def up_kernel(low_ref, up_ref, out_ref):
    chips = low_ref.shape[0]
    rank = up_ref.shape[1]
    zero = jnp.zeros((rank, 2 * LANES), BF)
    first = lax.broadcasted_iota(jnp.int32, (chips * 16, LANES), 0) % 16 < 8
    for pair in range(up_ref.shape[0] // 2):
        both = jnp.concatenate([up_ref[2 * pair], up_ref[2 * pair + 1]], axis=1)
        weight = jnp.concatenate(
            [jnp.concatenate([both, zero], axis=1), jnp.concatenate([zero, both], axis=1)], axis=0
        )
        x = low_ref[:, pair * 16:pair * 16 + 16, :].reshape(chips * 16, LANES)
        y = jnp.dot(x, weight, preferred_element_type=F32)
        for core in range(2):
            at = 2 * LANES * core
            delta = jnp.where(first, y[:, at:at + LANES], y[:, at + LANES:at + 2 * LANES]).astype(BF)
            out_ref[:, core, pair * 16:pair * 16 + 16, :] = delta.reshape(chips, 16, LANES)


def up_product(low, up):
    chips, slots, _ = low.shape
    return pl.pallas_call(
        up_kernel,
        in_specs=[whole(), whole()],
        out_specs=whole(),
        out_shape=jax.ShapeDtypeStruct((chips, 2, slots, LANES), BF),
        compiler_params=pltpu.CompilerParams(vmem_limit_bytes=24 << 20),
        cost_estimate=cost(2 * 1024 * 128 * 512, 1 << 20),
        name="up",
    )(low, up)


def full_path(tokens, ids_row, place_row, down, up, base):
    rows = tokens.shape[1]
    members = lax.axis_size("member")
    tensors = lax.axis_size("tensor")
    rank = up.shape[1]
    cap = 8
    rest = down.shape[0] * cap
    outbound, dest_row = dispatch(ids_row, place_row, tokens, members, cap)
    incoming = lax.all_to_all(outbound, "member", 0, 0, tiled=True)
    partial_low = down_product(incoming, down).reshape(tensors, 2 * rest, LANES)
    got = sum_and_spread(partial_low, rest, rank, tensors)
    delta = up_product(got, up).reshape(members, rest, LANES)
    back = lax.all_to_all(delta, "member", 0, 0, tiled=True).reshape(members * rest, LANES)
    return combine(dest_row.reshape(rows, 1), back, base)


def sum_and_spread(partial_low, rest, rank, tensors):
    shares = lax.all_to_all(partial_low, "tensor", 0, 0, tiled=True)
    low = jnp.sum(shares.astype(F32), axis=0).astype(BF)
    key = jnp.concatenate([low[:rest, :rank], low[rest:, :rank]], axis=1)
    val = jnp.concatenate([low[:rest, rank:], low[rest:, rank:]], axis=1)
    half = tensors // 2
    send = jnp.concatenate([
        jnp.broadcast_to(key[None], (half,) + key.shape),
        jnp.broadcast_to(val[None], (half,) + val.shape),
    ])
    return lax.all_to_all(send, "tensor", 0, 0, tiled=True)


FIT = 52
SENT = 56


def pack_kernel(ids_ref, place_ref, tokens_ref, out_ref, place56_ref, at_ref, dest_ref, meta_ref):
    rows = tokens_ref.shape[1]
    adapters = place_ref.shape[1]
    step = pl.program_id(0)
    lane8 = lax.broadcasted_iota(jnp.int32, (8, LANES), 1)
    sub8 = lax.broadcasted_iota(jnp.int32, (8, LANES), 0)

    @pl.when(step == 0)
    def _():
        number = lax.broadcasted_iota(jnp.int32, (adapters, rows), 0)
        hit = (number == ids_ref[...]).astype(F32).astype(BF)
        slot = jnp.dot(place_ref[...].astype(F32).astype(BF), hit, preferred_element_type=F32)[0:1].astype(jnp.int32)
        mine = (number == slot).astype(F32)
        earlier = lax.broadcasted_iota(jnp.int32, (rows, rows), 0) < lax.broadcasted_iota(jnp.int32, (rows, rows), 1)
        count = jnp.dot(mine.astype(BF), earlier.astype(F32).astype(BF), preferred_element_type=F32)
        total = jnp.broadcast_to(jnp.sum(mine, axis=1, keepdims=True), (adapters, LANES)).astype(BF)
        row = lax.broadcasted_iota(jnp.int32, (adapters, adapters), 0)
        col = lax.broadcasted_iota(jnp.int32, (adapters, adapters), 1)
        same = row // 8 == col // 8
        start = jnp.dot((same & (col < row)).astype(F32).astype(BF), total, preferred_element_type=F32)
        shifted = jnp.dot((same & (col % 8 < row % 8 - 4)).astype(F32).astype(BF), total, preferred_element_type=F32)
        place = jnp.sum(mine * (count + start[:, 0:1]), axis=0, keepdims=True).astype(jnp.int32)
        over = jnp.max((place >= FIT).astype(F32), axis=1, keepdims=True)
        lane = lax.broadcasted_iota(jnp.int32, (adapters, LANES), 1)
        sub = lax.broadcasted_iota(jnp.int32, (adapters, LANES), 0) % 8
        meta = jnp.where(lane < 64, shifted, start)
        meta_ref[...] = jnp.where((lane < 64) & (sub == 4), over, meta)
        owner = slot // 8
        dest_ref[...] = jnp.where(place < FIT, owner * 64 + place, -1)
        place56_ref[...] = jnp.where(place < FIT, owner * SENT + place, -1)
        at = lax.broadcasted_iota(jnp.int32, (256, rows), 0)
        inside = at % 64
        at = jnp.where(inside < FIT, at, jnp.where(inside < SENT, at - 4, -2))
        at_ref[...] = at.astype(F32).astype(BF)

    per_step = out_ref.shape[0]
    for part in range(per_step // 4):
        pick = one_hot(at_ref[...], within(dest_ref[...], step * per_step * 64 + part * 256))
        moved = lax.dot_general(pick, tokens_ref[...], (((1,), (1,)), ((), ())), preferred_element_type=F32)
        for d in range(4):
            own = moved[d * 64:(d + 1) * 64]
            owner = step * per_step + part * 4 + d
            meta = meta_ref[pl.ds(pl.multiple_of(owner * 8, 8), 8), :]
            third = jnp.concatenate([own[0:24, 256:320], own[24:48, 256:320]], axis=1)
            fourth = jnp.where(sub8 < 4, own[48:56, 0:128], own[48:56, 128:256])
            fifth = jnp.concatenate([own[48:56, 256:320], jnp.zeros((8, 64), F32)], axis=1)
            fifth = jnp.where(sub8 < 4, fifth, meta)
            out_ref[part * 4 + d] = jnp.concatenate(
                [own[0:48, 0:128], own[0:48, 128:256], third, fourth, fifth], axis=0
            ).astype(BF)


def pack(ids_row, place_row, tokens, members):
    feats, rows = tokens.shape
    per_step = 8
    return pl.pallas_call(
        pack_kernel,
        grid=(members // per_step,),
        in_specs=[
            pl.BlockSpec((1, rows), lambda i: (0, 0)),
            pl.BlockSpec(place_row.shape, lambda i: (0, 0)),
            pl.BlockSpec((feats, rows), lambda i: (0, 0)),
        ],
        out_specs=[
            pl.BlockSpec((per_step, 136, LANES), lambda i: (i, 0, 0)),
            pl.BlockSpec((1, rows), lambda i: (0, 0)),
        ],
        out_shape=[
            jax.ShapeDtypeStruct((members, 136, LANES), BF),
            jax.ShapeDtypeStruct((1, rows), jnp.int32),
        ],
        scratch_shapes=[pltpu.VMEM((256, rows), BF), pltpu.VMEM((1, rows), jnp.int32), pltpu.VMEM((256, LANES), F32)],
        compiler_params=pltpu.CompilerParams(vmem_limit_bytes=58 << 20),
        cost_estimate=cost(2 * 2048 * 1024 * 320, 3 << 20),
        name="pack",
    )(ids_row, place_row, tokens)


def short_down_kernel(in_ref, down_ref, out_ref, starts_ref, over_ref):
    members = in_ref.shape[0]
    x1 = in_ref[:, 0:48, :].reshape(members * 48, LANES)
    x2 = in_ref[:, 48:96, :].reshape(members * 48, LANES)
    tail = in_ref[:, 96:136, :].astype(F32)
    x3 = tail[:, 0:24].reshape(members * 24, LANES).astype(BF)
    x4 = tail[:, 24:32].reshape(members * 8, LANES).astype(BF)
    last = tail[:, 32:40].reshape(members * 8, LANES)
    lane = lax.broadcasted_iota(jnp.int32, (members * 8, LANES), 1)
    sub = lax.broadcasted_iota(jnp.int32, (members * 8, LANES), 0) % 8
    x5 = jnp.where(sub < 4, last, 0.0).astype(BF)
    turned = pltpu.roll(last, 64, 1)
    starts_ref[0] = jnp.where(lane < 64, last, turned).reshape(members, 8, LANES)
    starts_ref[1] = jnp.where(lane < 64, turned, last).reshape(members, 8, LANES)
    over_ref[...] = jnp.max(starts_ref[0, :, 4:5, :], axis=0)
    at = lax.broadcasted_iota(jnp.int32, (members, 48, LANES), 1).astype(F32)
    at_last = (lax.broadcasted_iota(jnp.int32, (members, 8, LANES), 1) % 4 + 48).astype(F32)
    zero = jnp.zeros((64, 2 * LANES), BF)
    low = low_last = None
    for pair in range(4):
        both = jnp.concatenate([down_ref[2 * pair], down_ref[2 * pair + 1]], axis=1)
        left = jnp.concatenate([both[256:320], zero], axis=0)
        right = jnp.concatenate([zero, both[256:320]], axis=0)
        y = jnp.dot(x1, both[0:128], preferred_element_type=F32)
        y += jnp.dot(x2, both[128:256], preferred_element_type=F32)
        thirds = [
            jnp.dot(x3, w, preferred_element_type=F32).reshape(members, 24, 2 * LANES) for w in (left, right)
        ]
        y = y.reshape(members, 48, 2 * LANES) + jnp.concatenate(thirds, axis=1)
        z1 = jnp.dot(x4, both[0:128], preferred_element_type=F32) + jnp.dot(x5, left, preferred_element_type=F32)
        z2 = jnp.dot(x4, both[128:256], preferred_element_type=F32)
        for n in range(2):
            adapter = 2 * pair + n
            lanes = slice(n * LANES, (n + 1) * LANES)
            z = jnp.where(sub < 4, z1[:, lanes], z2[:, lanes]).reshape(members, 8, LANES)
            if adapter == 0:
                low, low_last = y[:, :, lanes], z
            else:
                start = starts_ref[adapter // 4, :, 4 + adapter % 4:5 + adapter % 4, :]
                low = jnp.where(at >= start, y[:, :, lanes], low)
                low_last = jnp.where(at_last >= start, z, low_last)
    low_last = low_last.reshape(members * 8, LANES)
    low_last = jnp.where(sub < 4, low_last + pltpu.roll(low_last, members * 8 - 4, 0), 0.0)
    out_ref[...] = jnp.concatenate([low, low_last.reshape(members, 8, LANES)], axis=1).astype(BF)


def short_down(incoming, down):
    members = incoming.shape[0]
    return pl.pallas_call(
        short_down_kernel,
        in_specs=[whole(), whole()],
        out_specs=[whole()] * 3,
        out_shape=[
            jax.ShapeDtypeStruct((members, SENT, LANES), BF),
            jax.ShapeDtypeStruct((2, members, 8, LANES), F32),
            jax.ShapeDtypeStruct((1, LANES), F32),
        ],
        compiler_params=pltpu.CompilerParams(vmem_limit_bytes=32 << 20),
        cost_estimate=cost(3 * 10**10, 3 << 20),
        name="short_down",
    )(incoming, down)


def short_up_kernel(low_ref, up_ref, starts_ref, out_ref):
    chips = low_ref.shape[0]
    rank = up_ref.shape[1]
    x = low_ref[...].astype(F32).reshape(chips * SENT, LANES).astype(BF)
    zero = jnp.zeros((rank, 2 * LANES), BF)
    at = lax.broadcasted_iota(jnp.int32, (chips, SENT, LANES), 1).astype(F32)
    delta = [None, None]
    for pair in range(up_ref.shape[0] // 2):
        both = jnp.concatenate([up_ref[2 * pair], up_ref[2 * pair + 1]], axis=1)
        for core in range(2):
            weight = jnp.concatenate([both, zero] if core == 0 else [zero, both], axis=0)
            y = jnp.dot(x, weight, preferred_element_type=F32).reshape(chips, SENT, 2 * LANES)
            for n in range(2):
                adapter = 2 * pair + n
                own = y[:, :, n * LANES:(n + 1) * LANES]
                if adapter == 0:
                    delta[core] = own
                else:
                    start = starts_ref[adapter // 4, :, core, 4 + adapter % 4:5 + adapter % 4, :]
                    delta[core] = jnp.where(at >= start, own, delta[core])
    for core in range(2):
        out_ref[:, core] = delta[core].astype(BF)


def short_up(low, up, starts):
    chips = low.shape[0]
    return pl.pallas_call(
        short_up_kernel,
        in_specs=[whole()] * 3,
        out_specs=whole(),
        out_shape=jax.ShapeDtypeStruct((chips, 2, SENT, LANES), BF),
        compiler_params=pltpu.CompilerParams(vmem_limit_bytes=24 << 20),
        cost_estimate=cost(2 * 1024 * 128 * 512, 1 << 20),
        name="short_up",
    )(low, up, starts.reshape(2, chips, 2, 8, LANES))


def on_device(tokens, ids, place, base_weight, down, up):
    rows, feats = tokens.shape
    members = lax.axis_size("member")
    tensors = lax.axis_size("tensor")
    rank = up.shape[1]

    ids_row, place_row, tokens = ids.reshape(1, rows), place.reshape(1, -1), tokens.T
    outbound, place56 = pack(ids_row, place_row, tokens, members)
    incoming = lax.all_to_all(outbound, "member", 0, 0, tiled=True)

    def swapped(array, flip):
        return lax.ppermute(array, "tensor", [(t, t ^ flip) for t in range(tensors)])

    position = lax.axis_index("tensor").astype(jnp.int32).reshape(1)
    partials = base_product(position, place56, tokens, base_weight)
    along_x = [partials[0]] + [swapped(partials[k], k) for k in range(1, 4)]
    along_y = [partials[4]] + [swapped(partials[4 + l], 4 * l) for l in range(1, 4)]
    sums = first_sum(along_x + along_y)
    incoming, *sums = lax.optimization_barrier((incoming, *sums))
    then_y = [sums[0]] + [swapped(sums[l], 4 * l) for l in range(1, 4)]
    then_x = [sums[4]] + [swapped(sums[4 + k], k) for k in range(1, 4)]
    base = second_sum(then_y + then_x)

    partial_low, starts, over = short_down(incoming, down)
    got = sum_and_spread(partial_low.reshape(tensors, 2 * SENT, LANES), SENT, rank, tensors)
    delta = short_up(got, up, starts).reshape(members, SENT, LANES)
    back = lax.all_to_all(delta, "member", 0, 0, tiled=True).reshape(members * SENT, LANES)
    return lax.cond(
        over[0, 0] > 0.5,
        lambda: full_path(tokens, ids_row, place_row, down, up, base),
        lambda: combine(place56.reshape(rows, 1), back, base),
    )


def solution(mesh):
    in_specs = (
        P("member", "tensor"),
        P("member", None),
        P(),
        P("tensor", None),
        P("member", "tensor", None),
        P("member", None, "tensor"),
    )
    return jax.shard_map(on_device, mesh=mesh, in_specs=in_specs, out_specs=P("member", "tensor"), check_vma=False)
```

```python
import functools

import jax
import jax.numpy as jnp
from jax import lax
from jax.experimental import pallas as pl
from jax.experimental.pallas import tpu as pltpu
from jax.sharding import PartitionSpec as P

BF = jnp.bfloat16
F32 = jnp.float32
LANES = 128


def whole():
    return pl.BlockSpec(memory_space=pltpu.VMEM)


def cost(flops, size):
    return pl.CostEstimate(flops=flops, bytes_accessed=size, transcendentals=0)


def one_hot(at, index):
    return jnp.where(at == index, jnp.ones((), BF), jnp.zeros((), BF))


def within(dest, first):
    place = dest - first
    return jnp.where((place >= 0) & (place < 256), place, -1).astype(F32).astype(BF)


def dispatch_kernel(cap, ids_ref, place_ref, tokens_ref, out_ref, dest_ref, at_ref):
    rows = tokens_ref.shape[1]
    adapters = place_ref.shape[1]
    step = pl.program_id(0)

    @pl.when(step == 0)
    def _():
        hit = (lax.broadcasted_iota(jnp.int32, (adapters, rows), 0) == ids_ref[...]).astype(F32)
        before = lax.broadcasted_iota(jnp.int32, (rows, rows), 0) < lax.broadcasted_iota(jnp.int32, (rows, rows), 1)
        count = jnp.dot(hit.astype(BF), before.astype(F32).astype(BF), preferred_element_type=F32)
        rank = jnp.sum(hit * count, axis=0, keepdims=True)
        slot = jnp.dot(place_ref[...].astype(F32).astype(BF), hit.astype(BF), preferred_element_type=F32)
        dest_ref[...] = (slot[0:1] * cap + rank).astype(jnp.int32)
        at_ref[...] = lax.broadcasted_iota(jnp.int32, (256, rows), 0).astype(F32).astype(BF)

    width = 64
    per_step = out_ref.shape[0]
    for part in range(per_step * width // 256):
        pick = one_hot(at_ref[...], within(dest_ref[...], step * per_step * width + part * 256))
        moved = lax.dot_general(pick, tokens_ref[...], (((1,), (1,)), ((), ())), preferred_element_type=F32)
        for d in range(256 // width):
            own = moved[d * width:(d + 1) * width]
            to = part * (256 // width) + d
            out_ref[to, 0:64, :] = own[:, 0:128].astype(BF)
            out_ref[to, 64:128, :] = own[:, 128:256].astype(BF)
            out_ref[to, 128:160, :] = jnp.concatenate([own[0:32, 256:320], own[32:64, 256:320]], axis=1).astype(BF)


def dispatch(ids_row, place_row, tokens, members, cap):
    feats, rows = tokens.shape
    per_step = 8
    return pl.pallas_call(
        functools.partial(dispatch_kernel, cap),
        grid=(members // per_step,),
        in_specs=[
            pl.BlockSpec((1, rows), lambda i: (0, 0)),
            pl.BlockSpec(place_row.shape, lambda i: (0, 0)),
            pl.BlockSpec((feats, rows), lambda i: (0, 0)),
        ],
        out_specs=[
            pl.BlockSpec((per_step, 160, LANES), lambda i: (i, 0, 0)),
            pl.BlockSpec((1, rows), lambda i: (0, 0)),
        ],
        out_shape=[
            jax.ShapeDtypeStruct((members, 160, LANES), BF),
            jax.ShapeDtypeStruct((1, rows), jnp.int32),
        ],
        scratch_shapes=[pltpu.VMEM((256, rows), BF)],
        compiler_params=pltpu.CompilerParams(vmem_limit_bytes=58 << 20),
        cost_estimate=cost(2 * 2048 * 1024 * 320, 3 << 20),
        name="dispatch",
    )(ids_row, place_row, tokens)


def base_kernel(position_ref, dest_ref, tokens_ref, weight_ref, *out_refs):
    rows = tokens_ref[...].T
    half = rows.shape[0] // 2
    own = position_ref[0]
    odd = own % 2 == 1
    for pair in range(8):
        at = pl.multiple_of((own // 2 ^ pair) * 2 * LANES, 2 * LANES)
        y = jnp.dot(rows, weight_ref[:, pl.ds(at, 2 * LANES)], preferred_element_type=F32).astype(BF)
        for n in range(2):
            block = jnp.where(odd == (n == 1), y[:, :LANES], y[:, LANES:])
            l, k = divmod(2 * pair + n, 4)
            out_refs[k][l] = block[:half]
            out_refs[4 + l][k] = block[half:]


def base_product(position, dest_row, tokens, weight):
    feats, rows = tokens.shape
    cols = weight.shape[1]
    return pl.pallas_call(
        base_kernel,
        in_specs=[pl.BlockSpec(memory_space=pltpu.SMEM), whole(), whole(), whole()],
        out_specs=[whole()] * 8,
        out_shape=[jax.ShapeDtypeStruct((4, rows // 2, LANES), BF)] * 8,
        compiler_params=pltpu.CompilerParams(vmem_limit_bytes=24 << 20),
        cost_estimate=cost(2 * rows * feats * cols, 6 << 20),
        name="base",
    )(position, dest_row, tokens, weight)


def first_sum_kernel(*refs):
    for group in range(2):
        total = refs[4 * group][0].astype(F32)
        for ref in refs[4 * group + 1:4 * group + 4]:
            total += ref[0].astype(F32)
        entry = pl.program_id(0)
        for n in range(4):

            @pl.when(entry == n)
            def _(n=n, total=total, group=group):
                refs[8 + 4 * group + n][...] = total.astype(BF)


def first_sum(blocks):
    _, rows, _ = blocks[0].shape
    return pl.pallas_call(
        first_sum_kernel,
        grid=(4,),
        in_specs=[pl.BlockSpec((1, rows, LANES), lambda i: (i, 0, 0))] * 8,
        out_specs=[pl.BlockSpec((rows, LANES), lambda i: (0, 0))] * 8,
        out_shape=[jax.ShapeDtypeStruct((rows, LANES), BF)] * 8,
        compiler_params=pltpu.CompilerParams(vmem_limit_bytes=24 << 20),
        cost_estimate=cost(8 * rows * LANES * 4, 5 << 20),
        name="first_sum",
    )(*blocks)


def second_sum_kernel(*refs):
    rows = refs[0].shape[0]
    for group in range(2):
        total = refs[4 * group][...].astype(F32)
        for ref in refs[4 * group + 1:4 * group + 4]:
            total += ref[...].astype(F32)
        refs[8][group * rows:(group + 1) * rows, :] = total


def second_sum(blocks):
    rows = blocks[0].shape[0]
    return pl.pallas_call(
        second_sum_kernel,
        in_specs=[whole()] * 8,
        out_specs=whole(),
        out_shape=jax.ShapeDtypeStruct((2 * rows, LANES), F32),
        compiler_params=pltpu.CompilerParams(vmem_limit_bytes=16 << 20),
        cost_estimate=cost(8 * rows * LANES, 2 << 20),
        name="second_sum",
    )(*blocks)


def down_kernel(in_ref, down_ref, out_ref):
    members = in_ref.shape[0]
    zero = jnp.zeros((64, 2 * LANES), BF)
    first = lax.broadcasted_iota(jnp.int32, (members * 16, LANES), 0) % 16 < 8
    for pair in range(4):
        both = jnp.concatenate([down_ref[2 * pair], down_ref[2 * pair + 1]], axis=1)
        tail = [both[256:320], zero] if pair < 2 else [zero, both[256:320]]
        x1 = in_ref[:, pair * 16:pair * 16 + 16, :].reshape(members * 16, LANES)
        x2 = in_ref[:, 64 + pair * 16:80 + pair * 16, :].reshape(members * 16, LANES)
        third = 128 + (pair % 2) * 16
        x3 = in_ref[:, third:third + 16, :].reshape(members * 16, LANES)
        y = jnp.dot(x1, both[0:128], preferred_element_type=F32)
        y += jnp.dot(x2, both[128:256], preferred_element_type=F32)
        y += jnp.dot(x3, jnp.concatenate(tail, axis=0), preferred_element_type=F32)
        low = jnp.where(first, y[:, :LANES], y[:, LANES:]).astype(BF)
        out_ref[:, pair * 16:pair * 16 + 16, :] = low.reshape(members, 16, LANES)


def down_product(incoming, down):
    members = incoming.shape[0]
    return pl.pallas_call(
        down_kernel,
        in_specs=[whole(), whole()],
        out_specs=whole(),
        out_shape=jax.ShapeDtypeStruct((members, 64, LANES), BF),
        compiler_params=pltpu.CompilerParams(vmem_limit_bytes=24 << 20),
        cost_estimate=cost(3 * 10**10, 3 << 20),
        name="down",
    )(incoming, down)


def combine_kernel(dest_ref, delta_ref, base_ref, out_ref):
    rows = out_ref.shape[0]
    slots = delta_ref.shape[0]
    at = lax.broadcasted_iota(jnp.int32, (rows, 256), 1).astype(F32).astype(BF)
    total = base_ref[...].astype(F32)
    for part in range(slots // 256):
        pick = one_hot(at, within(dest_ref[...], part * 256))
        total += jnp.dot(pick, delta_ref[part * 256:(part + 1) * 256, :], preferred_element_type=F32)
    out_ref[...] = total.astype(out_ref.dtype)


def combine(dest_col, delta, base):
    rows = dest_col.shape[0]
    block = 512
    return pl.pallas_call(
        combine_kernel,
        grid=(rows // block,),
        in_specs=[
            pl.BlockSpec((block, 1), lambda i: (i, 0)),
            pl.BlockSpec(delta.shape, lambda i: (0, 0)),
            pl.BlockSpec((block, LANES), lambda i: (i, 0)),
        ],
        out_specs=pl.BlockSpec((block, LANES), lambda i: (i, 0)),
        out_shape=jax.ShapeDtypeStruct((rows, LANES), BF),
        compiler_params=pltpu.CompilerParams(vmem_limit_bytes=24 << 20),
        cost_estimate=cost(2 * rows * 2048 * LANES, 1 << 20),
        name="combine",
    )(dest_col, delta, base)


def up_kernel(low_ref, up_ref, out_ref):
    chips = low_ref.shape[0]
    rank = up_ref.shape[1]
    zero = jnp.zeros((rank, 2 * LANES), BF)
    first = lax.broadcasted_iota(jnp.int32, (chips * 16, LANES), 0) % 16 < 8
    for pair in range(up_ref.shape[0] // 2):
        both = jnp.concatenate([up_ref[2 * pair], up_ref[2 * pair + 1]], axis=1)
        weight = jnp.concatenate(
            [jnp.concatenate([both, zero], axis=1), jnp.concatenate([zero, both], axis=1)], axis=0
        )
        x = low_ref[:, pair * 16:pair * 16 + 16, :].reshape(chips * 16, LANES)
        y = jnp.dot(x, weight, preferred_element_type=F32)
        for core in range(2):
            at = 2 * LANES * core
            delta = jnp.where(first, y[:, at:at + LANES], y[:, at + LANES:at + 2 * LANES]).astype(BF)
            out_ref[:, core, pair * 16:pair * 16 + 16, :] = delta.reshape(chips, 16, LANES)


def up_product(low, up):
    chips, slots, _ = low.shape
    return pl.pallas_call(
        up_kernel,
        in_specs=[whole(), whole()],
        out_specs=whole(),
        out_shape=jax.ShapeDtypeStruct((chips, 2, slots, LANES), BF),
        compiler_params=pltpu.CompilerParams(vmem_limit_bytes=24 << 20),
        cost_estimate=cost(2 * 1024 * 128 * 512, 1 << 20),
        name="up",
    )(low, up)


def full_path(tokens, ids_row, place_row, down, up, base):
    rows = tokens.shape[1]
    members = lax.axis_size("member")
    tensors = lax.axis_size("tensor")
    rank = up.shape[1]
    cap = 8
    rest = down.shape[0] * cap
    outbound, dest_row = dispatch(ids_row, place_row, tokens, members, cap)
    incoming = lax.all_to_all(outbound, "member", 0, 0, tiled=True)
    partial_low = down_product(incoming, down).reshape(tensors, 2 * rest, LANES)
    got = sum_and_spread(partial_low, rest, rank, tensors)
    delta = up_product(got, up).reshape(members, rest, LANES)
    back = lax.all_to_all(delta, "member", 0, 0, tiled=True).reshape(members * rest, LANES)
    return combine(dest_row.reshape(rows, 1), back, base)


def sum_and_spread(partial_low, rest, rank, tensors):
    shares = lax.all_to_all(partial_low, "tensor", 0, 0, tiled=True)
    low = jnp.sum(shares.astype(F32), axis=0).astype(BF)
    key = jnp.concatenate([low[:rest, :rank], low[rest:, :rank]], axis=1)
    val = jnp.concatenate([low[:rest, rank:], low[rest:, rank:]], axis=1)
    half = tensors // 2
    send = jnp.concatenate([
        jnp.broadcast_to(key[None], (half,) + key.shape),
        jnp.broadcast_to(val[None], (half,) + val.shape),
    ])
    return lax.all_to_all(send, "tensor", 0, 0, tiled=True)


FIT = 52
SENT = 56


def pack_kernel(ids_ref, place_ref, tokens_hbm, out_ref, place56_ref, tokens_ref, at_ref, dest_ref, meta_ref, fetched):
    rows = tokens_hbm.shape[1]
    adapters = place_ref.shape[1]
    step = pl.program_id(0)
    sub8 = lax.broadcasted_iota(jnp.int32, (8, LANES), 0)

    @pl.when(step == 0)
    def _():
        fetch = pltpu.make_async_copy(tokens_hbm, tokens_ref, fetched)
        fetch.start()
        number = lax.broadcasted_iota(jnp.int32, (adapters, rows), 0)
        hit = (number == ids_ref[...]).astype(F32).astype(BF)
        slot = jnp.dot(place_ref[...].astype(F32).astype(BF), hit, preferred_element_type=F32)[0:1].astype(jnp.int32)
        mine = (number == slot).astype(F32)
        row = lax.broadcasted_iota(jnp.int32, (LANES, 2 * LANES), 0)
        col = lax.broadcasted_iota(jnp.int32, (LANES, 2 * LANES), 1)
        earlier = ((row < col) | (col >= LANES)).astype(F32).astype(BF)
        total = jnp.zeros((adapters, LANES), F32)
        counts = []
        for block in range(rows // LANES):
            own = mine[:, block * LANES:(block + 1) * LANES].astype(BF)
            both = jnp.dot(own, earlier, preferred_element_type=F32)
            counts.append(both[:, :LANES] + total)
            total += both[:, LANES:]
        total = total.astype(BF)
        row = lax.broadcasted_iota(jnp.int32, (adapters, adapters), 0)
        col = lax.broadcasted_iota(jnp.int32, (adapters, adapters), 1)
        same = row // 8 == col // 8
        start = jnp.dot((same & (col < row)).astype(F32).astype(BF), total, preferred_element_type=F32)
        shifted = jnp.dot((same & (col % 8 < row % 8 - 4)).astype(F32).astype(BF), total, preferred_element_type=F32)
        place = jnp.concatenate([
            jnp.sum(mine[:, n * LANES:(n + 1) * LANES] * (count + start), axis=0, keepdims=True)
            for n, count in enumerate(counts)
        ], axis=1).astype(jnp.int32)
        over = jnp.max((place >= FIT).astype(F32), axis=1, keepdims=True)
        lane = lax.broadcasted_iota(jnp.int32, (adapters, LANES), 1)
        sub = lax.broadcasted_iota(jnp.int32, (adapters, LANES), 0) % 8
        meta = jnp.where(lane < 64, shifted, start)
        meta_ref[...] = jnp.where((lane < 64) & (sub == 4), over, meta)
        owner = slot // 8
        dest_ref[...] = jnp.where(place < FIT, owner * 64 + place, -1)
        place56_ref[...] = jnp.where(place < FIT, owner * SENT + place, -1)
        at = lax.broadcasted_iota(jnp.int32, (256, rows), 0)
        inside = at % 64
        at = jnp.where(inside < FIT, at, jnp.where(inside < SENT, at - 4, -2))
        at_ref[...] = at.astype(F32).astype(BF)
        fetch.wait()

    per_step = out_ref.shape[0]
    for part in range(per_step // 4):
        pick = one_hot(at_ref[...], within(dest_ref[...], step * per_step * 64 + part * 256))
        moved = lax.dot_general(pick, tokens_ref[...], (((1,), (1,)), ((), ())), preferred_element_type=F32)
        for d in range(4):
            own = moved[d * 64:(d + 1) * 64]
            owner = step * per_step + part * 4 + d
            meta = meta_ref[pl.ds(pl.multiple_of(owner * 8, 8), 8), :]
            third = jnp.concatenate([own[0:24, 256:320], own[24:48, 256:320]], axis=1)
            fourth = jnp.where(sub8 < 4, own[48:56, 0:128], own[48:56, 128:256])
            fifth = jnp.concatenate([own[48:56, 256:320], jnp.zeros((8, 64), F32)], axis=1)
            fifth = jnp.where(sub8 < 4, fifth, meta)
            out_ref[part * 4 + d] = jnp.concatenate(
                [own[0:48, 0:128], own[0:48, 128:256], third, fourth, fifth], axis=0
            ).astype(BF)


def pack(ids_row, place_row, tokens, members):
    feats, rows = tokens.shape
    per_step = 8
    return pl.pallas_call(
        pack_kernel,
        grid=(members // per_step,),
        in_specs=[
            pl.BlockSpec((1, rows), lambda i: (0, 0)),
            pl.BlockSpec(place_row.shape, lambda i: (0, 0)),
            pl.BlockSpec(memory_space=pl.ANY),
        ],
        out_specs=[
            pl.BlockSpec((per_step, 136, LANES), lambda i: (i, 0, 0)),
            pl.BlockSpec((1, rows), lambda i: (0, 0)),
        ],
        out_shape=[
            jax.ShapeDtypeStruct((members, 136, LANES), BF),
            jax.ShapeDtypeStruct((1, rows), jnp.int32),
        ],
        scratch_shapes=[
            pltpu.VMEM((feats, rows), BF),
            pltpu.VMEM((256, rows), BF),
            pltpu.VMEM((1, rows), jnp.int32),
            pltpu.VMEM((256, LANES), F32),
            pltpu.SemaphoreType.DMA,
        ],
        compiler_params=pltpu.CompilerParams(vmem_limit_bytes=58 << 20),
        cost_estimate=cost(2 * 2048 * 1024 * 320, 3 << 20),
        name="pack",
    )(ids_row, place_row, tokens)


def short_down_kernel(in_ref, down_ref, out_ref, starts_ref, over_ref):
    members = in_ref.shape[0]
    x12 = jnp.concatenate([in_ref[:, 0:48, :], in_ref[:, 48:96, :]], axis=2).reshape(members * 48, 2 * LANES)
    tail = in_ref[:, 96:136, :].astype(F32)
    x3 = tail[:, 0:24].reshape(members * 24, LANES).astype(BF)
    x4 = tail[:, 24:32].reshape(members * 8, LANES).astype(BF)
    last = tail[:, 32:40].reshape(members * 8, LANES)
    lane = lax.broadcasted_iota(jnp.int32, (members * 8, LANES), 1)
    sub = lax.broadcasted_iota(jnp.int32, (members * 8, LANES), 0) % 8
    x5 = jnp.where(sub < 4, last, 0.0).astype(BF)
    x45 = jnp.concatenate([x4, x5], axis=1)
    turned = pltpu.roll(last, 64, 1)
    starts_ref[0] = jnp.where(lane < 64, last, turned).reshape(members, 8, LANES)
    starts_ref[1] = jnp.where(lane < 64, turned, last).reshape(members, 8, LANES)
    over_ref[...] = jnp.max(starts_ref[0, :, 4:5, :], axis=0)
    at = lax.broadcasted_iota(jnp.int32, (members, 48, LANES), 1).astype(F32)
    at_last = (lax.broadcasted_iota(jnp.int32, (members, 8, LANES), 1) % 4 + 48).astype(F32)
    zero = jnp.zeros((64, 2 * LANES), BF)
    low = low_last = None
    for pair in range(4):
        both = jnp.concatenate([down_ref[2 * pair], down_ref[2 * pair + 1]], axis=1)
        left = jnp.concatenate([both[256:320], zero], axis=0)
        right = jnp.concatenate([zero, both[256:320]], axis=0)
        y = jnp.dot(x12, both[0:256], preferred_element_type=F32)
        thirds = [
            jnp.dot(x3, w, preferred_element_type=F32).reshape(members, 24, 2 * LANES) for w in (left, right)
        ]
        y = y.reshape(members, 48, 2 * LANES) + jnp.concatenate(thirds, axis=1)
        z1 = jnp.dot(x45, jnp.concatenate([both[0:128], left], axis=0), preferred_element_type=F32)
        z2 = jnp.dot(x4, both[128:256], preferred_element_type=F32)
        for n in range(2):
            adapter = 2 * pair + n
            lanes = slice(n * LANES, (n + 1) * LANES)
            z = jnp.where(sub < 4, z1[:, lanes], z2[:, lanes]).reshape(members, 8, LANES)
            if adapter == 0:
                low, low_last = y[:, :, lanes], z
            else:
                start = starts_ref[adapter // 4, :, 4 + adapter % 4:5 + adapter % 4, :]
                low = jnp.where(at >= start, y[:, :, lanes], low)
                low_last = jnp.where(at_last >= start, z, low_last)
    low_last = low_last.reshape(members * 8, LANES)
    low_last = jnp.where(sub < 4, low_last + pltpu.roll(low_last, members * 8 - 4, 0), 0.0)
    out_ref[...] = jnp.concatenate([low, low_last.reshape(members, 8, LANES)], axis=1).astype(BF)


def short_down(incoming, down):
    members = incoming.shape[0]
    return pl.pallas_call(
        short_down_kernel,
        in_specs=[whole(), whole()],
        out_specs=[whole()] * 3,
        out_shape=[
            jax.ShapeDtypeStruct((members, SENT, LANES), BF),
            jax.ShapeDtypeStruct((2, members, 8, LANES), F32),
            jax.ShapeDtypeStruct((1, LANES), F32),
        ],
        compiler_params=pltpu.CompilerParams(vmem_limit_bytes=32 << 20),
        cost_estimate=cost(3 * 10**10, 3 << 20),
        name="short_down",
    )(incoming, down)


def short_up_kernel(low_ref, up_ref, starts_ref, out_ref):
    chips = low_ref.shape[0]
    rank = up_ref.shape[1]
    x = low_ref[...].astype(F32).reshape(chips * SENT, LANES).astype(BF)
    zero = jnp.zeros((rank, 2 * LANES), BF)
    at = lax.broadcasted_iota(jnp.int32, (chips, SENT, LANES), 1).astype(F32)
    delta = [None, None]
    for pair in range(up_ref.shape[0] // 2):
        both = jnp.concatenate([up_ref[2 * pair], up_ref[2 * pair + 1]], axis=1)
        for core in range(2):
            weight = jnp.concatenate([both, zero] if core == 0 else [zero, both], axis=0)
            y = jnp.dot(x, weight, preferred_element_type=F32).reshape(chips, SENT, 2 * LANES)
            for n in range(2):
                adapter = 2 * pair + n
                own = y[:, :, n * LANES:(n + 1) * LANES]
                if adapter == 0:
                    delta[core] = own
                else:
                    start = starts_ref[adapter // 4, :, core, 4 + adapter % 4:5 + adapter % 4, :]
                    delta[core] = jnp.where(at >= start, own, delta[core])
    for core in range(2):
        out_ref[:, core] = delta[core].astype(BF)


def short_up(low, up, starts):
    chips = low.shape[0]
    return pl.pallas_call(
        short_up_kernel,
        in_specs=[whole()] * 3,
        out_specs=whole(),
        out_shape=jax.ShapeDtypeStruct((chips, 2, SENT, LANES), BF),
        compiler_params=pltpu.CompilerParams(vmem_limit_bytes=24 << 20),
        cost_estimate=cost(2 * 1024 * 128 * 512, 1 << 20),
        name="short_up",
    )(low, up, starts.reshape(2, chips, 2, 8, LANES))


def on_device(tokens, ids, place, base_weight, down, up):
    rows, feats = tokens.shape
    members = lax.axis_size("member")
    tensors = lax.axis_size("tensor")
    rank = up.shape[1]

    ids_row, place_row, tokens = ids.reshape(1, rows), place.reshape(1, -1), tokens.T
    outbound, place56 = pack(ids_row, place_row, tokens, members)
    incoming = lax.all_to_all(outbound, "member", 0, 0, tiled=True)

    def swapped(array, flip):
        return lax.ppermute(array, "tensor", [(t, t ^ flip) for t in range(tensors)])

    position = lax.axis_index("tensor").astype(jnp.int32).reshape(1)
    partials = base_product(position, place56, tokens, base_weight)
    along_x = [partials[0]] + [swapped(partials[k], k) for k in range(1, 4)]
    along_y = [partials[4]] + [swapped(partials[4 + l], 4 * l) for l in range(1, 4)]
    sums = first_sum(along_x + along_y)
    incoming, *sums = lax.optimization_barrier((incoming, *sums))
    then_y = [sums[0]] + [swapped(sums[l], 4 * l) for l in range(1, 4)]
    then_x = [sums[4]] + [swapped(sums[4 + k], k) for k in range(1, 4)]
    base = second_sum(then_y + then_x)

    partial_low, starts, over = short_down(incoming, down)
    got = sum_and_spread(partial_low.reshape(tensors, 2 * SENT, LANES), SENT, rank, tensors)
    delta = short_up(got, up, starts).reshape(members, SENT, LANES)
    back = lax.all_to_all(delta, "member", 0, 0, tiled=True).reshape(members * SENT, LANES)
    return lax.cond(
        over[0, 0] > 0.5,
        lambda: full_path(tokens, ids_row, place_row, down, up, base),
        lambda: combine(place56.reshape(rows, 1), back, base),
    )


def solution(mesh):
    in_specs = (
        P("member", "tensor"),
        P("member", None),
        P(),
        P("tensor", None),
        P("member", "tensor", None),
        P("member", None, "tensor"),
    )
    return jax.shard_map(on_device, mesh=mesh, in_specs=in_specs, out_specs=P("member", "tensor"), check_vma=False)
```

```python
import functools

import jax
import jax.numpy as jnp
from jax import lax
from jax.experimental import pallas as pl
from jax.experimental.pallas import tpu as pltpu
from jax.sharding import PartitionSpec as P

BF = jnp.bfloat16
F32 = jnp.float32
LANES = 128


def whole():
    return pl.BlockSpec(memory_space=pltpu.VMEM)


def cost(flops, size):
    return pl.CostEstimate(flops=flops, bytes_accessed=size, transcendentals=0)


def one_hot(at, index):
    return jnp.where(at == index, jnp.ones((), BF), jnp.zeros((), BF))


def within(dest, first):
    place = dest - first
    return jnp.where((place >= 0) & (place < 256), place, -1).astype(F32).astype(BF)


def dispatch_kernel(cap, ids_ref, place_ref, tokens_ref, out_ref, dest_ref, at_ref):
    rows = tokens_ref.shape[1]
    adapters = place_ref.shape[1]
    step = pl.program_id(0)

    @pl.when(step == 0)
    def _():
        hit = (lax.broadcasted_iota(jnp.int32, (adapters, rows), 0) == ids_ref[...]).astype(F32)
        before = lax.broadcasted_iota(jnp.int32, (rows, rows), 0) < lax.broadcasted_iota(jnp.int32, (rows, rows), 1)
        count = jnp.dot(hit.astype(BF), before.astype(F32).astype(BF), preferred_element_type=F32)
        rank = jnp.sum(hit * count, axis=0, keepdims=True)
        slot = jnp.dot(place_ref[...].astype(F32).astype(BF), hit.astype(BF), preferred_element_type=F32)
        dest_ref[...] = (slot[0:1] * cap + rank).astype(jnp.int32)
        at_ref[...] = lax.broadcasted_iota(jnp.int32, (256, rows), 0).astype(F32).astype(BF)

    width = 64
    per_step = out_ref.shape[0]
    for part in range(per_step * width // 256):
        pick = one_hot(at_ref[...], within(dest_ref[...], step * per_step * width + part * 256))
        moved = lax.dot_general(pick, tokens_ref[...], (((1,), (1,)), ((), ())), preferred_element_type=F32)
        for d in range(256 // width):
            own = moved[d * width:(d + 1) * width]
            to = part * (256 // width) + d
            out_ref[to, 0:64, :] = own[:, 0:128].astype(BF)
            out_ref[to, 64:128, :] = own[:, 128:256].astype(BF)
            out_ref[to, 128:160, :] = jnp.concatenate([own[0:32, 256:320], own[32:64, 256:320]], axis=1).astype(BF)


def dispatch(ids_row, place_row, tokens, members, cap):
    feats, rows = tokens.shape
    per_step = 8
    return pl.pallas_call(
        functools.partial(dispatch_kernel, cap),
        grid=(members // per_step,),
        in_specs=[
            pl.BlockSpec((1, rows), lambda i: (0, 0)),
            pl.BlockSpec(place_row.shape, lambda i: (0, 0)),
            pl.BlockSpec((feats, rows), lambda i: (0, 0)),
        ],
        out_specs=[
            pl.BlockSpec((per_step, 160, LANES), lambda i: (i, 0, 0)),
            pl.BlockSpec((1, rows), lambda i: (0, 0)),
        ],
        out_shape=[
            jax.ShapeDtypeStruct((members, 160, LANES), BF),
            jax.ShapeDtypeStruct((1, rows), jnp.int32),
        ],
        scratch_shapes=[pltpu.VMEM((256, rows), BF)],
        compiler_params=pltpu.CompilerParams(vmem_limit_bytes=58 << 20),
        cost_estimate=cost(2 * 2048 * 1024 * 320, 3 << 20),
        name="dispatch",
    )(ids_row, place_row, tokens)


def base_kernel(position_ref, dest_ref, tokens_ref, weight_ref, *out_refs):
    rows = tokens_ref[...].T
    half = rows.shape[0] // 2
    own = position_ref[0]
    odd = own % 2 == 1
    for pair in range(8):
        at = pl.multiple_of((own // 2 ^ pair) * 2 * LANES, 2 * LANES)
        y = jnp.dot(rows, weight_ref[:, pl.ds(at, 2 * LANES)], preferred_element_type=F32).astype(BF)
        for n in range(2):
            block = jnp.where(odd == (n == 1), y[:, :LANES], y[:, LANES:])
            l, k = divmod(2 * pair + n, 4)
            out_refs[k][l] = block[:half]
            out_refs[4 + l][k] = block[half:]


def base_product(position, dest_row, tokens, weight):
    feats, rows = tokens.shape
    cols = weight.shape[1]
    return pl.pallas_call(
        base_kernel,
        in_specs=[pl.BlockSpec(memory_space=pltpu.SMEM), whole(), whole(), whole()],
        out_specs=[whole()] * 8,
        out_shape=[jax.ShapeDtypeStruct((4, rows // 2, LANES), BF)] * 8,
        compiler_params=pltpu.CompilerParams(vmem_limit_bytes=24 << 20),
        cost_estimate=cost(2 * rows * feats * cols, 6 << 20),
        name="base",
    )(position, dest_row, tokens, weight)


def first_sum_kernel(*refs):
    for group in range(2):
        total = refs[4 * group][0].astype(F32)
        for ref in refs[4 * group + 1:4 * group + 4]:
            total += ref[0].astype(F32)
        entry = pl.program_id(0)
        for n in range(4):

            @pl.when(entry == n)
            def _(n=n, total=total, group=group):
                refs[8 + 4 * group + n][...] = total.astype(BF)


def first_sum(blocks):
    _, rows, _ = blocks[0].shape
    return pl.pallas_call(
        first_sum_kernel,
        grid=(4,),
        in_specs=[pl.BlockSpec((1, rows, LANES), lambda i: (i, 0, 0))] * 8,
        out_specs=[pl.BlockSpec((rows, LANES), lambda i: (0, 0))] * 8,
        out_shape=[jax.ShapeDtypeStruct((rows, LANES), BF)] * 8,
        compiler_params=pltpu.CompilerParams(vmem_limit_bytes=24 << 20),
        cost_estimate=cost(8 * rows * LANES * 4, 5 << 20),
        name="first_sum",
    )(*blocks)


def second_sum_kernel(*refs):
    rows = refs[0].shape[0]
    for group in range(2):
        total = refs[4 * group][...].astype(F32)
        for ref in refs[4 * group + 1:4 * group + 4]:
            total += ref[...].astype(F32)
        refs[8][group * rows:(group + 1) * rows, :] = total


def second_sum(blocks):
    rows = blocks[0].shape[0]
    return pl.pallas_call(
        second_sum_kernel,
        in_specs=[whole()] * 8,
        out_specs=whole(),
        out_shape=jax.ShapeDtypeStruct((2 * rows, LANES), F32),
        compiler_params=pltpu.CompilerParams(vmem_limit_bytes=16 << 20),
        cost_estimate=cost(8 * rows * LANES, 2 << 20),
        name="second_sum",
    )(*blocks)


def down_kernel(in_ref, down_ref, out_ref):
    members = in_ref.shape[0]
    zero = jnp.zeros((64, 2 * LANES), BF)
    first = lax.broadcasted_iota(jnp.int32, (members * 16, LANES), 0) % 16 < 8
    for pair in range(4):
        both = jnp.concatenate([down_ref[2 * pair], down_ref[2 * pair + 1]], axis=1)
        tail = [both[256:320], zero] if pair < 2 else [zero, both[256:320]]
        x1 = in_ref[:, pair * 16:pair * 16 + 16, :].reshape(members * 16, LANES)
        x2 = in_ref[:, 64 + pair * 16:80 + pair * 16, :].reshape(members * 16, LANES)
        third = 128 + (pair % 2) * 16
        x3 = in_ref[:, third:third + 16, :].reshape(members * 16, LANES)
        y = jnp.dot(x1, both[0:128], preferred_element_type=F32)
        y += jnp.dot(x2, both[128:256], preferred_element_type=F32)
        y += jnp.dot(x3, jnp.concatenate(tail, axis=0), preferred_element_type=F32)
        low = jnp.where(first, y[:, :LANES], y[:, LANES:]).astype(BF)
        out_ref[:, pair * 16:pair * 16 + 16, :] = low.reshape(members, 16, LANES)


def down_product(incoming, down):
    members = incoming.shape[0]
    return pl.pallas_call(
        down_kernel,
        in_specs=[whole(), whole()],
        out_specs=whole(),
        out_shape=jax.ShapeDtypeStruct((members, 64, LANES), BF),
        compiler_params=pltpu.CompilerParams(vmem_limit_bytes=24 << 20),
        cost_estimate=cost(3 * 10**10, 3 << 20),
        name="down",
    )(incoming, down)


def marks_of(place):
    return within(place.reshape(-1, 1), 256 * jnp.arange(LANES, dtype=jnp.int32)[None, :])


def combine_kernel(marks_ref, delta_ref, base_ref, out_ref):
    rows = out_ref.shape[0]
    slots = delta_ref.shape[0]
    at = lax.broadcasted_iota(jnp.int32, (rows, 256), 1).astype(F32).astype(BF)
    total = base_ref[...].astype(F32)
    for part in range(slots // 256):
        pick = one_hot(at, marks_ref[:, part:part + 1])
        total += jnp.dot(pick, delta_ref[part * 256:(part + 1) * 256, :], preferred_element_type=F32)
    out_ref[...] = total.astype(out_ref.dtype)


def combine(marks, delta, base):
    rows = marks.shape[0]
    block = 512
    return pl.pallas_call(
        combine_kernel,
        grid=(rows // block,),
        in_specs=[
            pl.BlockSpec((block, LANES), lambda i: (i, 0)),
            pl.BlockSpec(delta.shape, lambda i: (0, 0)),
            pl.BlockSpec((block, LANES), lambda i: (i, 0)),
        ],
        out_specs=pl.BlockSpec((block, LANES), lambda i: (i, 0)),
        out_shape=pltpu.HBM((rows, LANES), BF),
        compiler_params=pltpu.CompilerParams(vmem_limit_bytes=24 << 20),
        cost_estimate=cost(2 * rows * 2048 * LANES, 1 << 20),
        name="combine",
    )(marks, delta, base)


def up_kernel(low_ref, up_ref, out_ref):
    chips = low_ref.shape[0]
    rank = up_ref.shape[1]
    zero = jnp.zeros((rank, 2 * LANES), BF)
    first = lax.broadcasted_iota(jnp.int32, (chips * 16, LANES), 0) % 16 < 8
    for pair in range(up_ref.shape[0] // 2):
        both = jnp.concatenate([up_ref[2 * pair], up_ref[2 * pair + 1]], axis=1)
        weight = jnp.concatenate(
            [jnp.concatenate([both, zero], axis=1), jnp.concatenate([zero, both], axis=1)], axis=0
        )
        x = low_ref[:, pair * 16:pair * 16 + 16, :].reshape(chips * 16, LANES)
        y = jnp.dot(x, weight, preferred_element_type=F32)
        for core in range(2):
            at = 2 * LANES * core
            delta = jnp.where(first, y[:, at:at + LANES], y[:, at + LANES:at + 2 * LANES]).astype(BF)
            out_ref[:, core, pair * 16:pair * 16 + 16, :] = delta.reshape(chips, 16, LANES)


def up_product(low, up):
    chips, slots, _ = low.shape
    return pl.pallas_call(
        up_kernel,
        in_specs=[whole(), whole()],
        out_specs=whole(),
        out_shape=jax.ShapeDtypeStruct((chips, 2, slots, LANES), BF),
        compiler_params=pltpu.CompilerParams(vmem_limit_bytes=24 << 20),
        cost_estimate=cost(2 * 1024 * 128 * 512, 1 << 20),
        name="up",
    )(low, up)


def full_path(tokens, ids_row, place_row, down, up, base):
    rows = tokens.shape[1]
    members = lax.axis_size("member")
    tensors = lax.axis_size("tensor")
    rank = up.shape[1]
    cap = 8
    rest = down.shape[0] * cap
    outbound, dest_row = dispatch(ids_row, place_row, tokens, members, cap)
    incoming = lax.all_to_all(outbound, "member", 0, 0, tiled=True)
    partial_low = down_product(incoming, down).reshape(tensors, 2 * rest, LANES)
    got = sum_and_spread(partial_low, rest, rank, tensors)
    delta = up_product(got, up).reshape(members, rest, LANES)
    back = lax.all_to_all(delta, "member", 0, 0, tiled=True).reshape(members * rest, LANES)
    return combine(marks_of(dest_row), back, base)


def sum_and_spread(partial_low, rest, rank, tensors):
    shares = lax.all_to_all(partial_low, "tensor", 0, 0, tiled=True)
    low = jnp.sum(shares.astype(F32), axis=0).astype(BF)
    key = jnp.concatenate([low[:rest, :rank], low[rest:, :rank]], axis=1)
    val = jnp.concatenate([low[:rest, rank:], low[rest:, rank:]], axis=1)
    half = tensors // 2
    send = jnp.concatenate([
        jnp.broadcast_to(key[None], (half,) + key.shape),
        jnp.broadcast_to(val[None], (half,) + val.shape),
    ])
    return lax.all_to_all(send, "tensor", 0, 0, tiled=True)


FIT = 52
SENT = 56


def pack_kernel(ids_ref, place_ref, tokens_hbm, out_ref, place56_ref, tokens_ref, at_ref, dest_ref, meta_ref, fetched):
    rows = tokens_hbm.shape[1]
    adapters = place_ref.shape[1]
    step = pl.program_id(0)
    sub8 = lax.broadcasted_iota(jnp.int32, (8, LANES), 0)

    @pl.when(step == 0)
    def _():
        fetch = pltpu.make_async_copy(tokens_hbm, tokens_ref, fetched)
        fetch.start()
        number = lax.broadcasted_iota(jnp.int32, (adapters, rows), 0)
        hit = (number == ids_ref[...]).astype(F32).astype(BF)
        slot = jnp.dot(place_ref[...].astype(F32).astype(BF), hit, preferred_element_type=F32)[0:1].astype(jnp.int32)
        mine = (number == slot).astype(F32)
        row = lax.broadcasted_iota(jnp.int32, (LANES, 2 * LANES), 0)
        col = lax.broadcasted_iota(jnp.int32, (LANES, 2 * LANES), 1)
        earlier = ((row < col) | (col >= LANES)).astype(F32).astype(BF)
        total = jnp.zeros((adapters, LANES), F32)
        counts = []
        for block in range(rows // LANES):
            own = mine[:, block * LANES:(block + 1) * LANES].astype(BF)
            both = jnp.dot(own, earlier, preferred_element_type=F32)
            counts.append(both[:, :LANES] + total)
            total += both[:, LANES:]
        total = total.astype(BF)
        row = lax.broadcasted_iota(jnp.int32, (adapters, adapters), 0)
        col = lax.broadcasted_iota(jnp.int32, (adapters, adapters), 1)
        same = row // 8 == col // 8
        start = jnp.dot((same & (col < row)).astype(F32).astype(BF), total, preferred_element_type=F32)
        shifted = jnp.dot((same & (col % 8 < row % 8 - 4)).astype(F32).astype(BF), total, preferred_element_type=F32)
        place = jnp.concatenate([
            jnp.sum(mine[:, n * LANES:(n + 1) * LANES] * (count + start), axis=0, keepdims=True)
            for n, count in enumerate(counts)
        ], axis=1).astype(jnp.int32)
        over = jnp.max((place >= FIT).astype(F32), axis=1, keepdims=True)
        lane = lax.broadcasted_iota(jnp.int32, (adapters, LANES), 1)
        sub = lax.broadcasted_iota(jnp.int32, (adapters, LANES), 0) % 8
        meta = jnp.where(lane < 64, shifted, start)
        meta_ref[...] = jnp.where((lane < 64) & (sub == 4), over, meta)
        owner = slot // 8
        dest_ref[...] = jnp.where(place < FIT, owner * 64 + place, -1)
        place56_ref[...] = jnp.where(place < FIT, owner * SENT + place, -1)
        at = lax.broadcasted_iota(jnp.int32, (256, rows), 0)
        inside = at % 64
        at = jnp.where(inside < FIT, at, jnp.where(inside < SENT, at - 4, -2))
        at_ref[...] = at.astype(F32).astype(BF)
        fetch.wait()

    per_step = out_ref.shape[0]
    for part in range(per_step // 4):
        pick = one_hot(at_ref[...], within(dest_ref[...], step * per_step * 64 + part * 256))
        moved = lax.dot_general(pick, tokens_ref[...], (((1,), (1,)), ((), ())), preferred_element_type=F32)
        for d in range(4):
            own = moved[d * 64:(d + 1) * 64]
            owner = step * per_step + part * 4 + d
            meta = meta_ref[pl.ds(pl.multiple_of(owner * 8, 8), 8), :]
            third = jnp.concatenate([own[0:24, 256:320], own[24:48, 256:320]], axis=1)
            fourth = jnp.where(sub8 < 4, own[48:56, 0:128], own[48:56, 128:256])
            fifth = jnp.concatenate([own[48:56, 256:320], jnp.zeros((8, 64), F32)], axis=1)
            fifth = jnp.where(sub8 < 4, fifth, meta)
            out_ref[part * 4 + d] = jnp.concatenate(
                [own[0:48, 0:128], own[0:48, 128:256], third, fourth, fifth], axis=0
            ).astype(BF)


def pack(ids_row, place_row, tokens, members):
    feats, rows = tokens.shape
    per_step = 8
    return pl.pallas_call(
        pack_kernel,
        grid=(members // per_step,),
        in_specs=[
            pl.BlockSpec((1, rows), lambda i: (0, 0)),
            pl.BlockSpec(place_row.shape, lambda i: (0, 0)),
            pl.BlockSpec(memory_space=pl.ANY),
        ],
        out_specs=[
            pl.BlockSpec((per_step, 136, LANES), lambda i: (i, 0, 0)),
            pl.BlockSpec((1, rows), lambda i: (0, 0)),
        ],
        out_shape=[
            jax.ShapeDtypeStruct((members, 136, LANES), BF),
            jax.ShapeDtypeStruct((1, rows), jnp.int32),
        ],
        scratch_shapes=[
            pltpu.VMEM((feats, rows), BF),
            pltpu.VMEM((256, rows), BF),
            pltpu.VMEM((1, rows), jnp.int32),
            pltpu.VMEM((256, LANES), F32),
            pltpu.SemaphoreType.DMA,
        ],
        compiler_params=pltpu.CompilerParams(vmem_limit_bytes=58 << 20),
        cost_estimate=cost(2 * 2048 * 1024 * 320, 3 << 20),
        name="pack",
    )(ids_row, place_row, tokens)


def short_down_kernel(in_ref, down_ref, out_ref, starts_ref, over_ref):
    members = in_ref.shape[0]
    x12 = jnp.concatenate([in_ref[:, 0:48, :], in_ref[:, 48:96, :]], axis=2).reshape(members * 48, 2 * LANES)
    tail = in_ref[:, 96:136, :].astype(F32)
    x3 = tail[:, 0:24].reshape(members * 24, LANES).astype(BF)
    x4 = tail[:, 24:32].reshape(members * 8, LANES).astype(BF)
    last = tail[:, 32:40].reshape(members * 8, LANES)
    lane = lax.broadcasted_iota(jnp.int32, (members * 8, LANES), 1)
    sub = lax.broadcasted_iota(jnp.int32, (members * 8, LANES), 0) % 8
    x5 = jnp.where(sub < 4, last, 0.0).astype(BF)
    x45 = jnp.concatenate([x4, x5], axis=1)
    turned = pltpu.roll(last, 64, 1)
    starts_ref[0] = jnp.where(lane < 64, last, turned).reshape(members, 8, LANES)
    starts_ref[1] = jnp.where(lane < 64, turned, last).reshape(members, 8, LANES)
    over_ref[...] = jnp.max(starts_ref[0, :, 4:5, :], axis=0)
    at = lax.broadcasted_iota(jnp.int32, (members, 48, LANES), 1).astype(F32)
    at_last = (lax.broadcasted_iota(jnp.int32, (members, 8, LANES), 1) % 4 + 48).astype(F32)
    zero = jnp.zeros((64, 2 * LANES), BF)
    low = low_last = None
    for pair in range(4):
        both = jnp.concatenate([down_ref[2 * pair], down_ref[2 * pair + 1]], axis=1)
        left = jnp.concatenate([both[256:320], zero], axis=0)
        right = jnp.concatenate([zero, both[256:320]], axis=0)
        y = jnp.dot(x12, both[0:256], preferred_element_type=F32)
        thirds = [
            jnp.dot(x3, w, preferred_element_type=F32).reshape(members, 24, 2 * LANES) for w in (left, right)
        ]
        y = y.reshape(members, 48, 2 * LANES) + jnp.concatenate(thirds, axis=1)
        z1 = jnp.dot(x45, jnp.concatenate([both[0:128], left], axis=0), preferred_element_type=F32)
        z2 = jnp.dot(x4, both[128:256], preferred_element_type=F32)
        for n in range(2):
            adapter = 2 * pair + n
            lanes = slice(n * LANES, (n + 1) * LANES)
            z = jnp.where(sub < 4, z1[:, lanes], z2[:, lanes]).reshape(members, 8, LANES)
            if adapter == 0:
                low, low_last = y[:, :, lanes], z
            else:
                start = starts_ref[adapter // 4, :, 4 + adapter % 4:5 + adapter % 4, :]
                low = jnp.where(at >= start, y[:, :, lanes], low)
                low_last = jnp.where(at_last >= start, z, low_last)
    low_last = low_last.reshape(members * 8, LANES)
    low_last = jnp.where(sub < 4, low_last + pltpu.roll(low_last, members * 8 - 4, 0), 0.0)
    out_ref[...] = jnp.concatenate([low, low_last.reshape(members, 8, LANES)], axis=1).astype(BF)


def short_down(incoming, down):
    members = incoming.shape[0]
    return pl.pallas_call(
        short_down_kernel,
        in_specs=[whole(), whole()],
        out_specs=[whole()] * 3,
        out_shape=[
            jax.ShapeDtypeStruct((members, SENT, LANES), BF),
            jax.ShapeDtypeStruct((2, members, 8, LANES), F32),
            jax.ShapeDtypeStruct((1, LANES), F32),
        ],
        compiler_params=pltpu.CompilerParams(vmem_limit_bytes=32 << 20),
        cost_estimate=cost(3 * 10**10, 3 << 20),
        name="short_down",
    )(incoming, down)


def short_up_kernel(low_ref, up_ref, starts_ref, out_ref):
    chips = low_ref.shape[0]
    rank = up_ref.shape[1]
    x = low_ref[...].astype(F32).reshape(chips * SENT, LANES).astype(BF)
    zero = jnp.zeros((rank, 2 * LANES), BF)
    at = lax.broadcasted_iota(jnp.int32, (chips, SENT, LANES), 1).astype(F32)
    delta = [None, None]
    for pair in range(up_ref.shape[0] // 2):
        both = jnp.concatenate([up_ref[2 * pair], up_ref[2 * pair + 1]], axis=1)
        for core in range(2):
            weight = jnp.concatenate([both, zero] if core == 0 else [zero, both], axis=0)
            y = jnp.dot(x, weight, preferred_element_type=F32).reshape(chips, SENT, 2 * LANES)
            for n in range(2):
                adapter = 2 * pair + n
                own = y[:, :, n * LANES:(n + 1) * LANES]
                if adapter == 0:
                    delta[core] = own
                else:
                    start = starts_ref[adapter // 4, :, core, 4 + adapter % 4:5 + adapter % 4, :]
                    delta[core] = jnp.where(at >= start, own, delta[core])
    for core in range(2):
        out_ref[:, core] = delta[core].astype(BF)


def short_up(low, up, starts):
    chips = low.shape[0]
    return pl.pallas_call(
        short_up_kernel,
        in_specs=[whole()] * 3,
        out_specs=whole(),
        out_shape=jax.ShapeDtypeStruct((chips, 2, SENT, LANES), BF),
        compiler_params=pltpu.CompilerParams(vmem_limit_bytes=24 << 20),
        cost_estimate=cost(2 * 1024 * 128 * 512, 1 << 20),
        name="short_up",
    )(low, up, starts.reshape(2, chips, 2, 8, LANES))


def on_device(tokens, ids, place, base_weight, down, up):
    rows, feats = tokens.shape
    members = lax.axis_size("member")
    tensors = lax.axis_size("tensor")
    rank = up.shape[1]

    ids_row, place_row, tokens = ids.reshape(1, rows), place.reshape(1, -1), tokens.T
    outbound, place56 = pack(ids_row, place_row, tokens, members)
    incoming = lax.all_to_all(outbound, "member", 0, 0, tiled=True)

    def swapped(array, flip):
        return lax.ppermute(array, "tensor", [(t, t ^ flip) for t in range(tensors)])

    position = lax.axis_index("tensor").astype(jnp.int32).reshape(1)
    partials = base_product(position, place56, tokens, base_weight)
    along_x = [partials[0]] + [swapped(partials[k], k) for k in range(1, 4)]
    along_y = [partials[4]] + [swapped(partials[4 + l], 4 * l) for l in range(1, 4)]
    sums = first_sum(along_x + along_y)
    incoming, *sums = lax.optimization_barrier((incoming, *sums))
    then_y = [sums[0]] + [swapped(sums[l], 4 * l) for l in range(1, 4)]
    then_x = [sums[4]] + [swapped(sums[4 + k], k) for k in range(1, 4)]
    base = second_sum(then_y + then_x)

    partial_low, starts, over = short_down(incoming, down)
    got = sum_and_spread(partial_low.reshape(tensors, 2 * SENT, LANES), SENT, rank, tensors)
    delta = short_up(got, up, starts).reshape(members, SENT, LANES)
    back = lax.all_to_all(delta, "member", 0, 0, tiled=True).reshape(members * SENT, LANES)
    return lax.cond(
        over[0, 0] > 0.5,
        lambda short: full_path(tokens, ids_row, place_row, down, up, base),
        lambda short: short,
        combine(marks_of(place56), back, base),
    )


def solution(mesh):
    in_specs = (
        P("member", "tensor"),
        P("member", None),
        P(),
        P("tensor", None),
        P("member", "tensor", None),
        P("member", None, "tensor"),
    )
    return jax.shard_map(on_device, mesh=mesh, in_specs=in_specs, out_specs=P("member", "tensor"), check_vma=False)
```

```python
import functools

import jax
import jax.numpy as jnp
from jax import lax
from jax.experimental import pallas as pl
from jax.experimental.pallas import tpu as pltpu
from jax.sharding import PartitionSpec as P

BF = jnp.bfloat16
F32 = jnp.float32
LANES = 128


def whole():
    return pl.BlockSpec(memory_space=pltpu.VMEM)


def cost(flops, size):
    return pl.CostEstimate(flops=flops, bytes_accessed=size, transcendentals=0)


def one_hot(at, index):
    return jnp.where(at == index, jnp.ones((), BF), jnp.zeros((), BF))


def within(dest, first):
    place = dest - first
    return jnp.where((place >= 0) & (place < 256), place, -1).astype(F32).astype(BF)


def dispatch_kernel(cap, ids_ref, place_ref, tokens_ref, out_ref, dest_ref, at_ref):
    rows = tokens_ref.shape[1]
    adapters = place_ref.shape[1]
    step = pl.program_id(0)

    @pl.when(step == 0)
    def _():
        hit = (lax.broadcasted_iota(jnp.int32, (adapters, rows), 0) == ids_ref[...]).astype(F32)
        before = lax.broadcasted_iota(jnp.int32, (rows, rows), 0) < lax.broadcasted_iota(jnp.int32, (rows, rows), 1)
        count = jnp.dot(hit.astype(BF), before.astype(F32).astype(BF), preferred_element_type=F32)
        rank = jnp.sum(hit * count, axis=0, keepdims=True)
        slot = jnp.dot(place_ref[...].astype(F32).astype(BF), hit.astype(BF), preferred_element_type=F32)
        dest_ref[...] = (slot[0:1] * cap + rank).astype(jnp.int32)
        at_ref[...] = lax.broadcasted_iota(jnp.int32, (256, rows), 0).astype(F32).astype(BF)

    width = 64
    per_step = out_ref.shape[0]
    for part in range(per_step * width // 256):
        pick = one_hot(at_ref[...], within(dest_ref[...], step * per_step * width + part * 256))
        moved = lax.dot_general(pick, tokens_ref[...], (((1,), (1,)), ((), ())), preferred_element_type=F32)
        for d in range(256 // width):
            own = moved[d * width:(d + 1) * width]
            to = part * (256 // width) + d
            out_ref[to, 0:64, :] = own[:, 0:128].astype(BF)
            out_ref[to, 64:128, :] = own[:, 128:256].astype(BF)
            out_ref[to, 128:160, :] = jnp.concatenate([own[0:32, 256:320], own[32:64, 256:320]], axis=1).astype(BF)


def dispatch(ids_row, place_row, tokens, members, cap):
    feats, rows = tokens.shape
    per_step = 8
    return pl.pallas_call(
        functools.partial(dispatch_kernel, cap),
        grid=(members // per_step,),
        in_specs=[
            pl.BlockSpec((1, rows), lambda i: (0, 0)),
            pl.BlockSpec(place_row.shape, lambda i: (0, 0)),
            pl.BlockSpec((feats, rows), lambda i: (0, 0)),
        ],
        out_specs=[
            pl.BlockSpec((per_step, 160, LANES), lambda i: (i, 0, 0)),
            pl.BlockSpec((1, rows), lambda i: (0, 0)),
        ],
        out_shape=[
            jax.ShapeDtypeStruct((members, 160, LANES), BF),
            jax.ShapeDtypeStruct((1, rows), jnp.int32),
        ],
        scratch_shapes=[pltpu.VMEM((256, rows), BF)],
        compiler_params=pltpu.CompilerParams(vmem_limit_bytes=58 << 20),
        cost_estimate=cost(2 * 2048 * 1024 * 320, 3 << 20),
        name="dispatch",
    )(ids_row, place_row, tokens)


def base_kernel(position_ref, dest_ref, tokens_ref, weight_ref, *out_refs):
    rows = tokens_ref[...].T
    half = rows.shape[0] // 2
    own = position_ref[0]
    odd = own % 2 == 1
    for pair in range(8):
        at = pl.multiple_of((own // 2 ^ pair) * 2 * LANES, 2 * LANES)
        y = jnp.dot(rows, weight_ref[:, pl.ds(at, 2 * LANES)], preferred_element_type=F32).astype(BF)
        for n in range(2):
            block = jnp.where(odd == (n == 1), y[:, :LANES], y[:, LANES:])
            l, k = divmod(2 * pair + n, 4)
            out_refs[k][l] = block[:half]
            out_refs[4 + l][k] = block[half:]


def base_product(position, dest_row, tokens, weight):
    feats, rows = tokens.shape
    cols = weight.shape[1]
    return pl.pallas_call(
        base_kernel,
        in_specs=[pl.BlockSpec(memory_space=pltpu.SMEM), whole(), whole(), whole()],
        out_specs=[whole()] * 8,
        out_shape=[jax.ShapeDtypeStruct((4, rows // 2, LANES), BF)] * 8,
        compiler_params=pltpu.CompilerParams(vmem_limit_bytes=24 << 20),
        cost_estimate=cost(2 * rows * feats * cols, 6 << 20),
        name="base",
    )(position, dest_row, tokens, weight)


def first_sum_kernel(*refs):
    for group in range(2):
        total = refs[4 * group][0].astype(F32)
        for ref in refs[4 * group + 1:4 * group + 4]:
            total += ref[0].astype(F32)
        entry = pl.program_id(0)
        for n in range(4):

            @pl.when(entry == n)
            def _(n=n, total=total, group=group):
                refs[8 + 4 * group + n][...] = total.astype(BF)


def first_sum(blocks):
    _, rows, _ = blocks[0].shape
    return pl.pallas_call(
        first_sum_kernel,
        grid=(4,),
        in_specs=[pl.BlockSpec((1, rows, LANES), lambda i: (i, 0, 0))] * 8,
        out_specs=[pl.BlockSpec((rows, LANES), lambda i: (0, 0))] * 8,
        out_shape=[jax.ShapeDtypeStruct((rows, LANES), BF)] * 8,
        compiler_params=pltpu.CompilerParams(vmem_limit_bytes=24 << 20),
        cost_estimate=cost(8 * rows * LANES * 4, 5 << 20),
        name="first_sum",
    )(*blocks)


def second_sum_kernel(*refs):
    rows = refs[0].shape[0]
    for group in range(2):
        total = refs[4 * group][...].astype(F32)
        for ref in refs[4 * group + 1:4 * group + 4]:
            total += ref[...].astype(F32)
        refs[8][group * rows:(group + 1) * rows, :] = total


def second_sum(blocks):
    rows = blocks[0].shape[0]
    return pl.pallas_call(
        second_sum_kernel,
        in_specs=[whole()] * 8,
        out_specs=whole(),
        out_shape=jax.ShapeDtypeStruct((2 * rows, LANES), F32),
        compiler_params=pltpu.CompilerParams(vmem_limit_bytes=16 << 20),
        cost_estimate=cost(8 * rows * LANES, 2 << 20),
        name="second_sum",
    )(*blocks)


def down_kernel(in_ref, down_ref, out_ref):
    members = in_ref.shape[0]
    zero = jnp.zeros((64, 2 * LANES), BF)
    first = lax.broadcasted_iota(jnp.int32, (members * 16, LANES), 0) % 16 < 8
    for pair in range(4):
        both = jnp.concatenate([down_ref[2 * pair], down_ref[2 * pair + 1]], axis=1)
        tail = [both[256:320], zero] if pair < 2 else [zero, both[256:320]]
        x1 = in_ref[:, pair * 16:pair * 16 + 16, :].reshape(members * 16, LANES)
        x2 = in_ref[:, 64 + pair * 16:80 + pair * 16, :].reshape(members * 16, LANES)
        third = 128 + (pair % 2) * 16
        x3 = in_ref[:, third:third + 16, :].reshape(members * 16, LANES)
        y = jnp.dot(x1, both[0:128], preferred_element_type=F32)
        y += jnp.dot(x2, both[128:256], preferred_element_type=F32)
        y += jnp.dot(x3, jnp.concatenate(tail, axis=0), preferred_element_type=F32)
        low = jnp.where(first, y[:, :LANES], y[:, LANES:]).astype(BF)
        out_ref[:, pair * 16:pair * 16 + 16, :] = low.reshape(members, 16, LANES)


def down_product(incoming, down):
    members = incoming.shape[0]
    return pl.pallas_call(
        down_kernel,
        in_specs=[whole(), whole()],
        out_specs=whole(),
        out_shape=jax.ShapeDtypeStruct((members, 64, LANES), BF),
        compiler_params=pltpu.CompilerParams(vmem_limit_bytes=24 << 20),
        cost_estimate=cost(3 * 10**10, 3 << 20),
        name="down",
    )(incoming, down)


def marks_of(place):
    return within(place.reshape(-1, 1), 256 * jnp.arange(LANES, dtype=jnp.int32)[None, :])


def combine_kernel(marks_ref, delta_ref, base_ref, out_ref):
    rows = out_ref.shape[0]
    slots = delta_ref.shape[0]
    at = lax.broadcasted_iota(jnp.int32, (rows, 256), 1).astype(F32).astype(BF)
    own = pl.ds(pl.multiple_of(pl.program_id(0) * rows, rows), rows)
    marks = marks_ref[own, :]
    total = base_ref[own, :].astype(F32)
    for part in range(slots // 256):
        pick = one_hot(at, marks[:, part:part + 1])
        total += jnp.dot(pick, delta_ref[part * 256:(part + 1) * 256, :], preferred_element_type=F32)
    out_ref[...] = total.astype(out_ref.dtype)


def combine(marks, delta, base):
    rows = marks.shape[0]
    block = 256
    return pl.pallas_call(
        combine_kernel,
        grid=(rows // block,),
        in_specs=[whole()] * 3,
        out_specs=pl.BlockSpec((block, LANES), lambda i: (i, 0)),
        out_shape=pltpu.HBM((rows, LANES), BF),
        compiler_params=pltpu.CompilerParams(vmem_limit_bytes=24 << 20),
        cost_estimate=cost(2 * rows * 2048 * LANES, 1 << 20),
        name="combine",
    )(marks, delta, base)


def up_kernel(low_ref, up_ref, out_ref):
    chips = low_ref.shape[0]
    rank = up_ref.shape[1]
    zero = jnp.zeros((rank, 2 * LANES), BF)
    first = lax.broadcasted_iota(jnp.int32, (chips * 16, LANES), 0) % 16 < 8
    for pair in range(up_ref.shape[0] // 2):
        both = jnp.concatenate([up_ref[2 * pair], up_ref[2 * pair + 1]], axis=1)
        weight = jnp.concatenate(
            [jnp.concatenate([both, zero], axis=1), jnp.concatenate([zero, both], axis=1)], axis=0
        )
        x = low_ref[:, pair * 16:pair * 16 + 16, :].reshape(chips * 16, LANES)
        y = jnp.dot(x, weight, preferred_element_type=F32)
        for core in range(2):
            at = 2 * LANES * core
            delta = jnp.where(first, y[:, at:at + LANES], y[:, at + LANES:at + 2 * LANES]).astype(BF)
            out_ref[:, core, pair * 16:pair * 16 + 16, :] = delta.reshape(chips, 16, LANES)


def up_product(low, up):
    chips, slots, _ = low.shape
    return pl.pallas_call(
        up_kernel,
        in_specs=[whole(), whole()],
        out_specs=whole(),
        out_shape=jax.ShapeDtypeStruct((chips, 2, slots, LANES), BF),
        compiler_params=pltpu.CompilerParams(vmem_limit_bytes=24 << 20),
        cost_estimate=cost(2 * 1024 * 128 * 512, 1 << 20),
        name="up",
    )(low, up)


def full_path(tokens, ids_row, place_row, down, up, base):
    rows = tokens.shape[1]
    members = lax.axis_size("member")
    tensors = lax.axis_size("tensor")
    rank = up.shape[1]
    cap = 8
    rest = down.shape[0] * cap
    outbound, dest_row = dispatch(ids_row, place_row, tokens, members, cap)
    incoming = lax.all_to_all(outbound, "member", 0, 0, tiled=True)
    partial_low = down_product(incoming, down).reshape(tensors, 2 * rest, LANES)
    got = sum_and_spread(partial_low, rest, rank, tensors)
    delta = up_product(got, up).reshape(members, rest, LANES)
    back = lax.all_to_all(delta, "member", 0, 0, tiled=True).reshape(members * rest, LANES)
    return combine(marks_of(dest_row), back, base)


def sum_and_spread(partial_low, rest, rank, tensors):
    shares = lax.all_to_all(partial_low, "tensor", 0, 0, tiled=True)
    low = jnp.sum(shares.astype(F32), axis=0).astype(BF)
    key = jnp.concatenate([low[:rest, :rank], low[rest:, :rank]], axis=1)
    val = jnp.concatenate([low[:rest, rank:], low[rest:, rank:]], axis=1)
    half = tensors // 2
    send = jnp.concatenate([
        jnp.broadcast_to(key[None], (half,) + key.shape),
        jnp.broadcast_to(val[None], (half,) + val.shape),
    ])
    return lax.all_to_all(send, "tensor", 0, 0, tiled=True)


FIT = 52
SENT = 56


def pack_kernel(ids_ref, place_ref, tokens_hbm, out_ref, place56_ref, tokens_ref, at_ref, dest_ref, meta_ref, fetched):
    rows = tokens_hbm.shape[1]
    adapters = place_ref.shape[1]
    step = pl.program_id(0)
    sub8 = lax.broadcasted_iota(jnp.int32, (8, LANES), 0)

    @pl.when(step == 0)
    def _():
        fetch = pltpu.make_async_copy(tokens_hbm, tokens_ref, fetched)
        fetch.start()
        number = lax.broadcasted_iota(jnp.int32, (adapters, rows), 0)
        hit = (number == ids_ref[...]).astype(F32).astype(BF)
        slot = jnp.dot(place_ref[...].astype(F32).astype(BF), hit, preferred_element_type=F32)[0:1].astype(jnp.int32)
        mine = (number == slot).astype(F32)
        row = lax.broadcasted_iota(jnp.int32, (LANES, 2 * LANES), 0)
        col = lax.broadcasted_iota(jnp.int32, (LANES, 2 * LANES), 1)
        earlier = ((row < col) | (col >= LANES)).astype(F32).astype(BF)
        total = jnp.zeros((adapters, LANES), F32)
        counts = []
        for block in range(rows // LANES):
            own = mine[:, block * LANES:(block + 1) * LANES].astype(BF)
            both = jnp.dot(own, earlier, preferred_element_type=F32)
            counts.append(both[:, :LANES] + total)
            total += both[:, LANES:]
        total = total.astype(BF)
        row = lax.broadcasted_iota(jnp.int32, (adapters, adapters), 0)
        col = lax.broadcasted_iota(jnp.int32, (adapters, adapters), 1)
        same = row // 8 == col // 8
        start = jnp.dot((same & (col < row)).astype(F32).astype(BF), total, preferred_element_type=F32)
        shifted = jnp.dot((same & (col % 8 < row % 8 - 4)).astype(F32).astype(BF), total, preferred_element_type=F32)
        place = jnp.concatenate([
            jnp.sum(mine[:, n * LANES:(n + 1) * LANES] * (count + start), axis=0, keepdims=True)
            for n, count in enumerate(counts)
        ], axis=1).astype(jnp.int32)
        over = jnp.max((place >= FIT).astype(F32), axis=1, keepdims=True)
        lane = lax.broadcasted_iota(jnp.int32, (adapters, LANES), 1)
        sub = lax.broadcasted_iota(jnp.int32, (adapters, LANES), 0) % 8
        meta = jnp.where(lane < 64, shifted, start)
        meta_ref[...] = jnp.where((lane < 64) & (sub == 4), over, meta)
        owner = slot // 8
        dest_ref[...] = jnp.where(place < FIT, owner * 64 + place, -1)
        place56_ref[...] = jnp.where(place < FIT, owner * SENT + place, -1)
        at = lax.broadcasted_iota(jnp.int32, (256, rows), 0)
        inside = at % 64
        at = jnp.where(inside < FIT, at, jnp.where(inside < SENT, at - 4, -2))
        at_ref[...] = at.astype(F32).astype(BF)
        fetch.wait()

    per_step = out_ref.shape[0]
    for part in range(per_step // 4):
        pick = one_hot(at_ref[...], within(dest_ref[...], step * per_step * 64 + part * 256))
        moved = lax.dot_general(pick, tokens_ref[...], (((1,), (1,)), ((), ())), preferred_element_type=F32)
        for d in range(4):
            own = moved[d * 64:(d + 1) * 64]
            owner = step * per_step + part * 4 + d
            meta = meta_ref[pl.ds(pl.multiple_of(owner * 8, 8), 8), :]
            third = jnp.concatenate([own[0:24, 256:320], own[24:48, 256:320]], axis=1)
            fourth = jnp.where(sub8 < 4, own[48:56, 0:128], own[48:56, 128:256])
            fifth = jnp.concatenate([own[48:56, 256:320], jnp.zeros((8, 64), F32)], axis=1)
            fifth = jnp.where(sub8 < 4, fifth, meta)
            out_ref[part * 4 + d] = jnp.concatenate(
                [own[0:48, 0:128], own[0:48, 128:256], third, fourth, fifth], axis=0
            ).astype(BF)


def pack(ids_row, place_row, tokens, members):
    feats, rows = tokens.shape
    per_step = 8
    return pl.pallas_call(
        pack_kernel,
        grid=(members // per_step,),
        in_specs=[
            pl.BlockSpec((1, rows), lambda i: (0, 0)),
            pl.BlockSpec(place_row.shape, lambda i: (0, 0)),
            pl.BlockSpec(memory_space=pl.ANY),
        ],
        out_specs=[
            pl.BlockSpec((per_step, 136, LANES), lambda i: (i, 0, 0)),
            pl.BlockSpec((1, rows), lambda i: (0, 0)),
        ],
        out_shape=[
            jax.ShapeDtypeStruct((members, 136, LANES), BF),
            jax.ShapeDtypeStruct((1, rows), jnp.int32),
        ],
        scratch_shapes=[
            pltpu.VMEM((feats, rows), BF),
            pltpu.VMEM((256, rows), BF),
            pltpu.VMEM((1, rows), jnp.int32),
            pltpu.VMEM((256, LANES), F32),
            pltpu.SemaphoreType.DMA,
        ],
        compiler_params=pltpu.CompilerParams(vmem_limit_bytes=58 << 20),
        cost_estimate=cost(2 * 2048 * 1024 * 320, 3 << 20),
        name="pack",
    )(ids_row, place_row, tokens)


def short_down_kernel(in_ref, down_ref, out_ref, starts_ref, over_ref):
    members = in_ref.shape[0]
    x12 = jnp.concatenate([in_ref[:, 0:48, :], in_ref[:, 48:96, :]], axis=2).reshape(members * 48, 2 * LANES)
    tail = in_ref[:, 96:136, :].astype(F32)
    x3 = tail[:, 0:24].reshape(members * 24, LANES).astype(BF)
    x4 = tail[:, 24:32].reshape(members * 8, LANES).astype(BF)
    last = tail[:, 32:40].reshape(members * 8, LANES)
    lane = lax.broadcasted_iota(jnp.int32, (members * 8, LANES), 1)
    sub = lax.broadcasted_iota(jnp.int32, (members * 8, LANES), 0) % 8
    x5 = jnp.where(sub < 4, last, 0.0).astype(BF)
    x45 = jnp.concatenate([x4, x5], axis=1)
    turned = pltpu.roll(last, 64, 1)
    starts_ref[0] = jnp.where(lane < 64, last, turned).reshape(members, 8, LANES)
    starts_ref[1] = jnp.where(lane < 64, turned, last).reshape(members, 8, LANES)
    over_ref[...] = jnp.max(starts_ref[0, :, 4:5, :], axis=0)
    at = lax.broadcasted_iota(jnp.int32, (members, 48, LANES), 1).astype(F32)
    at_last = (lax.broadcasted_iota(jnp.int32, (members, 8, LANES), 1) % 4 + 48).astype(F32)
    zero = jnp.zeros((64, 2 * LANES), BF)
    low = low_last = None
    for pair in range(4):
        both = jnp.concatenate([down_ref[2 * pair], down_ref[2 * pair + 1]], axis=1)
        left = jnp.concatenate([both[256:320], zero], axis=0)
        right = jnp.concatenate([zero, both[256:320]], axis=0)
        y = jnp.dot(x12, both[0:256], preferred_element_type=F32)
        thirds = [
            jnp.dot(x3, w, preferred_element_type=F32).reshape(members, 24, 2 * LANES) for w in (left, right)
        ]
        y = y.reshape(members, 48, 2 * LANES) + jnp.concatenate(thirds, axis=1)
        z1 = jnp.dot(x45, jnp.concatenate([both[0:128], left], axis=0), preferred_element_type=F32)
        z2 = jnp.dot(x4, both[128:256], preferred_element_type=F32)
        for n in range(2):
            adapter = 2 * pair + n
            lanes = slice(n * LANES, (n + 1) * LANES)
            z = jnp.where(sub < 4, z1[:, lanes], z2[:, lanes]).reshape(members, 8, LANES)
            if adapter == 0:
                low, low_last = y[:, :, lanes], z
            else:
                start = starts_ref[adapter // 4, :, 4 + adapter % 4:5 + adapter % 4, :]
                low = jnp.where(at >= start, y[:, :, lanes], low)
                low_last = jnp.where(at_last >= start, z, low_last)
    low_last = low_last.reshape(members * 8, LANES)
    low_last = jnp.where(sub < 4, low_last + pltpu.roll(low_last, members * 8 - 4, 0), 0.0)
    out_ref[...] = jnp.concatenate([low, low_last.reshape(members, 8, LANES)], axis=1).astype(BF)


def short_down(incoming, down):
    members = incoming.shape[0]
    return pl.pallas_call(
        short_down_kernel,
        in_specs=[whole(), whole()],
        out_specs=[whole()] * 3,
        out_shape=[
            jax.ShapeDtypeStruct((members, SENT, LANES), BF),
            jax.ShapeDtypeStruct((2, members, 8, LANES), F32),
            jax.ShapeDtypeStruct((1, LANES), F32),
        ],
        compiler_params=pltpu.CompilerParams(vmem_limit_bytes=32 << 20),
        cost_estimate=cost(3 * 10**10, 3 << 20),
        name="short_down",
    )(incoming, down)


def short_up_kernel(low_ref, up_ref, starts_ref, out_ref):
    chips = low_ref.shape[0]
    rank = up_ref.shape[1]
    x = low_ref[...].astype(F32).reshape(chips * SENT, LANES).astype(BF)
    zero = jnp.zeros((rank, 2 * LANES), BF)
    at = lax.broadcasted_iota(jnp.int32, (chips, SENT, LANES), 1).astype(F32)
    delta = [None, None]
    for pair in range(up_ref.shape[0] // 2):
        both = jnp.concatenate([up_ref[2 * pair], up_ref[2 * pair + 1]], axis=1)
        for core in range(2):
            weight = jnp.concatenate([both, zero] if core == 0 else [zero, both], axis=0)
            y = jnp.dot(x, weight, preferred_element_type=F32).reshape(chips, SENT, 2 * LANES)
            for n in range(2):
                adapter = 2 * pair + n
                own = y[:, :, n * LANES:(n + 1) * LANES]
                if adapter == 0:
                    delta[core] = own
                else:
                    start = starts_ref[adapter // 4, :, core, 4 + adapter % 4:5 + adapter % 4, :]
                    delta[core] = jnp.where(at >= start, own, delta[core])
    for core in range(2):
        out_ref[:, core] = delta[core].astype(BF)


def short_up(low, up, starts):
    chips = low.shape[0]
    return pl.pallas_call(
        short_up_kernel,
        in_specs=[whole()] * 3,
        out_specs=whole(),
        out_shape=jax.ShapeDtypeStruct((chips, 2, SENT, LANES), BF),
        compiler_params=pltpu.CompilerParams(vmem_limit_bytes=24 << 20),
        cost_estimate=cost(2 * 1024 * 128 * 512, 1 << 20),
        name="short_up",
    )(low, up, starts.reshape(2, chips, 2, 8, LANES))


def on_device(tokens, ids, place, base_weight, down, up):
    rows, feats = tokens.shape
    members = lax.axis_size("member")
    tensors = lax.axis_size("tensor")
    rank = up.shape[1]

    ids_row, place_row, tokens = ids.reshape(1, rows), place.reshape(1, -1), tokens.T
    outbound, place56 = pack(ids_row, place_row, tokens, members)
    incoming = lax.all_to_all(outbound, "member", 0, 0, tiled=True)

    def swapped(array, flip):
        return lax.ppermute(array, "tensor", [(t, t ^ flip) for t in range(tensors)])

    position = lax.axis_index("tensor").astype(jnp.int32).reshape(1)
    partials = base_product(position, place56, tokens, base_weight)
    along_x = [partials[0]] + [swapped(partials[k], k) for k in range(1, 4)]
    along_y = [partials[4]] + [swapped(partials[4 + l], 4 * l) for l in range(1, 4)]
    sums = first_sum(along_x + along_y)
    incoming, *sums = lax.optimization_barrier((incoming, *sums))
    then_y = [sums[0]] + [swapped(sums[l], 4 * l) for l in range(1, 4)]
    then_x = [sums[4]] + [swapped(sums[4 + k], k) for k in range(1, 4)]
    base = second_sum(then_y + then_x)

    partial_low, starts, over = short_down(incoming, down)
    got = sum_and_spread(partial_low.reshape(tensors, 2 * SENT, LANES), SENT, rank, tensors)
    delta = short_up(got, up, starts).reshape(members, SENT, LANES)
    back = lax.all_to_all(delta, "member", 0, 0, tiled=True).reshape(members * SENT, LANES)
    return lax.cond(
        over[0, 0] > 0.5,
        lambda short: full_path(tokens, ids_row, place_row, down, up, base),
        lambda short: short,
        combine(marks_of(place56), back, base),
    )


def solution(mesh):
    in_specs = (
        P("member", "tensor"),
        P("member", None),
        P(),
        P("tensor", None),
        P("member", "tensor", None),
        P("member", None, "tensor"),
    )
    return jax.shard_map(on_device, mesh=mesh, in_specs=in_specs, out_specs=P("member", "tensor"), check_vma=False)
```
